32 devices in a mesh: grp: 1, date: 16 (over z, y, x), tile: 2 (over core).
Axes of the slice: x: 2, y: 2, z: 4, core: 2. Of those that a mesh axis runs over, the one named last changes fastest.
Arguments:
- acquisitions: bfloat16 [2, 64, 32, 8192], P(None, 'date', 'grp', 'tile'), may hold values from -102 to 102
- pair_list: int32 [960, 2], P('date'), may hold values from -1 to 63, as said below
- win_rows: int32 [8], replicated, may hold values from 1 to 8
- win_cols: int32 [1], replicated, may hold values from 18 to 32
Outputs:
- coherence: float32 [2, 960, 8, 512], P(None, 'date', 'grp', 'tile')
The draws below stay inside these ranges and needn't reach their ends.
Inputs may be any that keep to these rules, and one draw needn't show every extreme that they name: `pair_list`: the 60 slots of one owner (one index of date) list pairs (i, j) whose first date i is held by that owner, with i < j <= i + 15; each pair stands once; live slots come first and unused slots hold -1 in both columns; some owner has all slots live.
All inputs are finite; a program needn't handle non-finite values.
Results may differ from the reference program's by a relative error of at most 0.0013.
Values may be sent and summed in bfloat16 or wider, within the bound.
A program may use at most 64 MiB of HBM per device.

```python
import math
import jax
import jax.numpy as jnp
from jax import lax

DATE_DEV = 4
ROWS = 32
SPAN = 15
STRIDE_R = 4
STRIDE_C = 16
DATES = 64
COLS = 8192
PAIR_DEV = 60
PAIRS = 960
OR = 8
OC = 512


def draw_acquisitions(key, part):
    key = jax.random.fold_in(key, 11)
    subkeys = jax.random.split(key, 6)
    scene = jnp.clip(jax.random.normal(subkeys[0], (2, 1, ROWS, COLS), jnp.float32), -4.0, 4.0)
    noise = jnp.clip(jax.random.normal(subkeys[1], (2, DATES, ROWS, COLS), jnp.float32), -4.0, 4.0)
    mixing = jnp.exp(jax.random.uniform(subkeys[2], (1, DATES, 1, 1), jnp.float32, math.log(0.3), math.log(3.0)))
    texture = jnp.exp(0.5 * jnp.clip(jax.random.normal(subkeys[3], (1, 1, ROWS, COLS), jnp.float32), -3.0, 3.0))
    phase_rate = jax.random.uniform(subkeys[4], (DATES, 1, 1), jnp.float32, -0.05, 0.05)
    phase_base = jax.random.uniform(subkeys[5], (DATES, 1, 1), jnp.float32, -math.pi, math.pi)
    column_index = jnp.arange(COLS, dtype=jnp.float32)
    phase_map = phase_base + phase_rate * column_index
    mixed = texture * (scene + mixing * noise)
    cosine = jnp.cos(phase_map)
    sine_map = jnp.sin(phase_map)
    real_part = mixed[0] * cosine - mixed[1] * sine_map
    imag_part = mixed[0] * sine_map + mixed[1] * cosine
    return jnp.stack([real_part, imag_part]).astype(jnp.bfloat16)


def draw_pair_list(key, part):
    key = jax.random.fold_in(key, 23)
    owners = DATES // DATE_DEV
    date_index = jnp.arange(DATES, dtype=jnp.int32)
    partners = jax.random.randint(key, (DATES,), 1, SPAN + 1, dtype=jnp.int32)
    partners = jnp.where(date_index < DATE_DEV, SPAN, partners)
    partners = jnp.minimum(partners, DATES - 1 - date_index)
    counts = partners.reshape(owners, DATE_DEV)
    inclusive = jnp.cumsum(counts, axis=1)
    exclusive = inclusive - counts
    slot_index = jnp.arange(PAIR_DEV, dtype=jnp.int32)
    local_date = jnp.sum((inclusive[:, None, :] <= slot_index[None, :, None]).astype(jnp.int32), axis=2)
    live_slot = slot_index[None, :] < inclusive[:, -1:]
    clipped = jnp.minimum(local_date, DATE_DEV - 1)
    start_slot = jnp.take_along_axis(exclusive, clipped, axis=1)
    first_date = jnp.arange(owners, dtype=jnp.int32)[:, None] * DATE_DEV + clipped
    second_date = first_date + slot_index[None, :] - start_slot + 1
    entries = jnp.stack([first_date, second_date], axis=-1)
    entries = jnp.where(live_slot[:, :, None], entries, -1)
    return entries.reshape(PAIRS, 2).astype(jnp.int32)


def place_ends(drawn, key, least, top_value):
    shape = drawn.shape
    place = [jax.random.randint(jax.random.fold_in(key, axis), (), 0, shape[axis]) for axis in range(len(shape))]
    drawn = drawn.at[tuple(place)].set(least)
    longest = shape.index(max(shape))
    place[longest] = (place[longest] + 1) % shape[longest]
    return drawn.at[tuple(place)].set(top_value)


def setup_inputs(seed: int = 0, part: int = 0) -> dict:
    key_of = jax.random.split(jax.random.key(seed), 5)
    own_keys = jax.random.split(jax.random.fold_in(key_of[4], part), 5)
    acquisitions = draw_acquisitions(jax.random.fold_in(jax.random.fold_in(key_of[4], part), 71), part)
    pair_list = draw_pair_list(jax.random.fold_in(key_of[4], 71), part)
    win_rows = place_ends(jax.random.randint(key_of[2], (OR,), 1, 2 * STRIDE_R + 1), jax.random.fold_in(key_of[2], 1), 1, 2 * STRIDE_R).astype(jnp.int32)
    win_cols = jax.random.randint(key_of[3], (1,), STRIDE_C + 2, 2 * STRIDE_C + 1).astype(jnp.int32)
    return {"acquisitions": acquisitions, "pair_list": pair_list, "win_rows": win_rows, "win_cols": win_cols}


EPS = 1e-06

def column_weights(win_cols):
    offsets = jnp.arange(2 * STRIDE_C, dtype=jnp.int32)
    return (jnp.abs(2 * offsets + 1 - 2 * STRIDE_C) <= win_cols[0]).astype(jnp.float32)

def row_weights(win_rows):
    out_index = lax.broadcasted_iota(jnp.int32, (OR, ROWS), 0)
    row_index = lax.broadcasted_iota(jnp.int32, (OR, ROWS), 1)
    return (jnp.abs(2 * row_index + 1 - (2 * out_index + 1) * STRIDE_R) <= win_rows[:, None]).astype(jnp.float32)

def multilook(field_stack, col_taps, row_taps):
    count = field_stack.shape[0]
    half_cols = STRIDE_C // 2
    widened = jnp.pad(field_stack.astype(jnp.float32), ((0, 0), (0, 0), (half_cols, half_cols)))
    lead_part = widened[:, :, :OC * STRIDE_C].reshape(count, ROWS, OC, STRIDE_C)
    tail_part = widened[:, :, STRIDE_C:STRIDE_C + OC * STRIDE_C].reshape(count, ROWS, OC, STRIDE_C)
    blocks = jnp.concatenate([lead_part, tail_part], axis=3)
    summed = lax.optimization_barrier(jnp.sum(blocks * col_taps, axis=3))
    return jnp.einsum('or,brk->bok', row_taps, summed, precision=lax.Precision.HIGHEST)

def reference(acquisitions, pair_list, win_rows, win_cols):
    col_taps = column_weights(win_cols)
    row_taps = row_weights(win_rows)
    real_part = acquisitions[0].astype(jnp.float32)
    imag_part = acquisitions[1].astype(jnp.float32)
    power_map = (real_part * real_part + imag_part * imag_part).astype(jnp.bfloat16)
    looked_power = multilook(power_map, col_taps, row_taps)

    def one_pair(pair_entry):
        first_date = jnp.maximum(pair_entry[0], 0).astype(jnp.int32)
        second_date = jnp.maximum(pair_entry[1], 0).astype(jnp.int32)
        lead_tile = lax.dynamic_index_in_dim(acquisitions, first_date, 1, keepdims=False).astype(jnp.float32)
        other_tile = lax.dynamic_index_in_dim(acquisitions, second_date, 1, keepdims=False).astype(jnp.float32)
        product_real = (lead_tile[0] * other_tile[0] + lead_tile[1] * other_tile[1]).astype(jnp.bfloat16)
        product_imag = (lead_tile[1] * other_tile[0] - lead_tile[0] * other_tile[1]).astype(jnp.bfloat16)
        looked = multilook(jnp.stack([product_real, product_imag]), col_taps, row_taps)
        power_first = lax.dynamic_index_in_dim(looked_power, first_date, 0, keepdims=False)
        power_second = lax.dynamic_index_in_dim(looked_power, second_date, 0, keepdims=False)
        denominator = jnp.sqrt(power_first * power_second + EPS)
        return jnp.where(pair_entry[0] >= 0, looked / denominator, jnp.zeros_like(looked))
    result = lax.map(one_pair, pair_list)
    return jnp.transpose(result, (1, 0, 2, 3))
```

```python
import functools

import jax
import jax.numpy as jnp
import numpy as np
from jax import lax
from jax.experimental import pallas as pl
from jax.experimental.pallas import tpu as pltpu
from jax.sharding import PartitionSpec as P

SPAN = 15
STRIDE_R = 4
STRIDE_C = 16
EPS = 1e-06

GROUP = 4
OWN = 4
LOCAL = GROUP * OWN
DOWN = 8
UP_FROM = DOWN + 1
UP = LOCAL - UP_FROM
HELD = LOCAL + DOWN + UP
HALF = STRIDE_C // 2
LANES = 128
CHUNK = 16
MESH = pl.DeviceIdType.MESH


def pair_plan():
    first, second, counts, ups = [], [], [], []
    place = np.zeros((GROUP, OWN * SPAN), np.int32)
    near = [min(SPAN, LOCAL + DOWN - 1 - i) for i in range(LOCAL)]
    for member in range(GROUP):
        at = 0
        for step in range(OWN):
            i = member * OWN + step
            for d in range(near[i]):
                first.append(i)
                second.append(i + 1 + d)
                place[member, step * SPAN + d] = at
                at += 1
        counts.append(at)
        for step in range(OWN):
            i = member * OWN + step
            for d in range(near[i], SPAN):
                place[member, step * SPAN + d] = at
                at += 1
        ups.append(at - counts[-1])
    for member in range(GROUP):
        for step in range(OWN):
            i = member * OWN + step
            for d in range(near[i], SPAN):
                first.append(LOCAL + DOWN + i - UP_FROM)
                second.append(i + 1 + d - LOCAL)
    return np.array(first, np.int32), np.array(second, np.int32), counts, ups, place


FIRST, SECOND, COUNTS, UPS, PLACE = pair_plan()
TOTAL = len(FIRST)
STARTS = [sum(COUNTS[:k]) for k in range(GROUP)]
UP_STARTS = [sum(COUNTS) + sum(UPS[:k]) for k in range(GROUP)]


def other_member(member, k):
    if k == 1:
        return member + 1 - 2 * (member % 2)
    if k == 2:
        return member + 2 - 4 * (member // 2)
    return GROUP - 1 - member


def spread_kernel(groups, width, acq, rim, held, send, recv, far_send, far_recv, local):
    date = lax.axis_index("date")
    group, member = date // GROUP, date % GROUP
    base = group * GROUP
    has_before, has_after = group > 0, group < groups - 1

    barrier = pltpu.get_barrier_semaphore()
    for k in (1, 2, 3):
        pl.semaphore_signal(
            barrier, inc=1, device_id={"date": base + other_member(member, k)}, device_id_type=MESH
        )

    @pl.when(has_before)
    def _():
        pl.semaphore_signal(barrier, inc=1, device_id={"date": date - GROUP}, device_id_type=MESH)

    @pl.when(has_after)
    def _():
        pl.semaphore_signal(barrier, inc=1, device_id={"date": date + GROUP}, device_id_type=MESH)

    peers = GROUP - 1 + has_before.astype(jnp.int32) + has_after.astype(jnp.int32)
    pl.semaphore_wait(barrier, peers)

    def body_of(who):
        return acq.at[:, :, :, pl.ds(pl.multiple_of(who * width, width), width)]

    def rim_of(who):
        return rim.at[who]

    def slot(start, count):
        part = held.at[:, pl.ds(start, count)]
        return part.at[:, :, :, pl.ds(0, width)], part.at[:, :, :, pl.ds(width, LANES)]

    near = []
    for k in (1, 2, 3):
        who = other_member(member, k)
        main, side = slot(member * OWN, OWN)
        pair = [
            pltpu.make_async_remote_copy(
                src_ref=src,
                dst_ref=dst,
                send_sem=send.at[k, n],
                recv_sem=recv.at[k, n],
                device_id={"date": base + who},
                device_id_type=MESH,
            )
            for n, (src, dst) in enumerate(((body_of(who), main), (rim_of(who), side)))
        ]
        for copy in pair:
            copy.start()
        near.append(pair)
    main, side = slot(member * OWN, OWN)
    mine = [
        pltpu.make_async_copy(body_of(member), main, local.at[0]),
        pltpu.make_async_copy(rim_of(member), side, local.at[1]),
    ]
    for copy in mine:
        copy.start()

    onward = [
        (0, OWN, LOCAL, -1),
        (OWN, OWN, LOCAL + OWN, -1),
        (UP_FROM, 3 * OWN - UP_FROM, LOCAL + DOWN, 1),
        (3 * OWN, OWN, LOCAL + DOWN + 3 * OWN - UP_FROM, 1),
    ]

    def far(source):
        start, count, place, step = onward[source]
        return pltpu.make_async_remote_copy(
            src_ref=held.at[:, pl.ds(start, count)],
            dst_ref=held.at[:, pl.ds(place, count)],
            send_sem=far_send.at[source],
            recv_sem=far_recv.at[source],
            device_id={"date": date + step * GROUP},
            device_id_type=MESH,
        )

    def pass_on(who):
        for source in range(GROUP):
            exists = has_before if onward[source][3] < 0 else has_after

            @pl.when(jnp.logical_and(who == source, exists))
            def _():
                far(source).start()

    for copy in mine:
        copy.wait()
    pass_on(member)
    for k in (1, 2, 3):
        for copy in near[k - 1]:
            copy.wait_recv()
        pass_on(other_member(member, k))
    for pair in near:
        for copy in pair:
            copy.wait_send()

    for source in range(GROUP):
        start, count, place, step = onward[source]
        sends = has_before if step < 0 else has_after
        gets = has_after if step < 0 else has_before

        @pl.when(sends)
        def _():
            far(source).wait_send()

        @pl.when(gets)
        def _():
            far(source).wait_recv()

        @pl.when(jnp.logical_not(gets))
        def _():
            fill = pltpu.make_async_copy(
                held.at[:, pl.ds(start, count)], held.at[:, pl.ds(place, count)], local.at[2]
            )
            fill.start()
            fill.wait()


def spread(acq, rim, groups):
    width = acq.shape[3] // GROUP
    return pl.pallas_call(
        functools.partial(spread_kernel, groups, width),
        out_shape=jax.ShapeDtypeStruct((2, HELD, acq.shape[2], width + LANES), acq.dtype),
        in_specs=[pl.BlockSpec(memory_space=pl.ANY)] * 2,
        out_specs=pl.BlockSpec(memory_space=pl.ANY),
        scratch_shapes=[
            pltpu.SemaphoreType.DMA((GROUP, 2)),
            pltpu.SemaphoreType.DMA((GROUP, 2)),
            pltpu.SemaphoreType.DMA((GROUP,)),
            pltpu.SemaphoreType.DMA((GROUP,)),
            pltpu.SemaphoreType.DMA((3,)),
        ],
        compiler_params=pltpu.CompilerParams(collective_id=0, has_side_effects=True),
        name="spread",
    )(acq, rim)


def split_dot(taps, values):
    high = values.astype(jnp.bfloat16)
    low = (values - high.astype(jnp.float32)).astype(jnp.bfloat16)
    return jnp.dot(taps, high, preferred_element_type=jnp.float32) + jnp.dot(
        taps, low, preferred_element_type=jnp.float32
    )


def pairs_kernel(
    rows, width, first, second, win_rows, win_cols, held, result, product, col_taps, row_taps, power
):
    out_rows = rows // STRIDE_R
    out_cols = width // STRIDE_C
    full = width + LANES
    step = pl.program_id(0)
    cuts = [(r, c) for r in range(0, rows, 16) for c in range(0, full, 384)]

    @pl.when(step == 0)
    def _():
        lane = lax.broadcasted_iota(jnp.int32, (full, LANES), 0)
        out = lax.broadcasted_iota(jnp.int32, (full, LANES), 1) % out_cols
        column = jnp.where(
            lane < width, lane, jnp.where(lane < width + HALF, lane - width - HALF, lane - HALF)
        )
        near = jnp.abs(2 * column + 1 - (2 * out + 1) * STRIDE_C) <= win_cols[0]
        near = jnp.logical_and(near, lane < width + 2 * HALF)
        col_taps[...] = jnp.where(near, 1.0, 0.0).astype(jnp.bfloat16)

        shape = (CHUNK * out_rows, CHUNK * rows)
        at = lax.broadcasted_iota(jnp.int32, shape, 0)
        row = lax.broadcasted_iota(jnp.int32, shape, 1)
        window = jnp.zeros(shape, jnp.int32)
        for o in range(out_rows):
            window = jnp.where(at % out_rows == o, win_rows[o], window)
        inside = jnp.abs(2 * (row % rows) + 1 - (2 * (at % out_rows) + 1) * STRIDE_R) <= window
        inside = jnp.logical_and(inside, at // out_rows == row // rows)
        row_taps[...] = jnp.where(inside, 1.0, 0.0).astype(jnp.bfloat16)

        def one_date(d, carry):
            for r, c in cuts:
                re = held[0, d, r : r + 16, c : c + 384].astype(jnp.float32)
                im = held[1, d, r : r + 16, c : c + 384].astype(jnp.float32)
                at = pl.multiple_of(d * rows + r, 16)
                product[pl.ds(at, 16), c : c + 384] = (re * re + im * im).astype(jnp.bfloat16)
            return carry

        lax.fori_loop(0, HELD, one_date, 0)
        product[HELD * rows :] = jnp.zeros((2 * CHUNK * rows - HELD * rows, full), jnp.bfloat16)
        across = jnp.dot(product[...], col_taps[...], preferred_element_type=jnp.float32)
        half = CHUNK * rows
        for n in range(2):
            looked = split_dot(row_taps[...], across[n * half : (n + 1) * half])
            power[n * CHUNK : (n + 1) * CHUNK] = looked.reshape(CHUNK, out_rows, LANES)

    def one_pair(p, carry):
        i = first[step * CHUNK + p]
        j = second[step * CHUNK + p]
        for r, c in cuts:
            re_i = held[0, i, r : r + 16, c : c + 384].astype(jnp.float32)
            im_i = held[1, i, r : r + 16, c : c + 384].astype(jnp.float32)
            re_j = held[0, j, r : r + 16, c : c + 384].astype(jnp.float32)
            im_j = held[1, j, r : r + 16, c : c + 384].astype(jnp.float32)
            at = pl.multiple_of(p * 2 * rows + r, 16)
            product[pl.ds(at, 16), c : c + 384] = (re_i * re_j + im_i * im_j).astype(jnp.bfloat16)
            at = pl.multiple_of(p * 2 * rows + rows + r, 16)
            product[pl.ds(at, 16), c : c + 384] = (im_i * re_j - re_i * im_j).astype(jnp.bfloat16)
        return carry

    lax.fori_loop(0, CHUNK, one_pair, 0)
    across = jnp.dot(product[...], col_taps[...], preferred_element_type=jnp.float32)
    across = across.reshape(CHUNK, 2, rows, LANES)
    lane = lax.broadcasted_iota(jnp.int32, (CHUNK, rows, LANES), 2)
    both = jnp.where(lane < out_cols, across[:, 0], across[:, 1]).reshape(CHUNK * rows, LANES)
    looked = split_dot(row_taps[...], both).reshape(CHUNK, out_rows, LANES)
    for p in range(CHUNK):
        i = first[step * CHUNK + p]
        j = second[step * CHUNK + p]
        result[p] = looked[p] * lax.rsqrt(power[i] * power[j] + EPS)


def work_pairs(held, win_rows, win_cols):
    rows, full = held.shape[2:]
    width = full - LANES
    out_rows = rows // STRIDE_R
    smem = pl.BlockSpec(memory_space=pltpu.SMEM)
    return pl.pallas_call(
        functools.partial(pairs_kernel, rows, width),
        grid=(TOTAL // CHUNK,),
        out_shape=jax.ShapeDtypeStruct((TOTAL, out_rows, LANES), jnp.float32),
        in_specs=[smem, smem, smem, smem, pl.BlockSpec(held.shape, lambda s: (0, 0, 0, 0))],
        out_specs=pl.BlockSpec((CHUNK, out_rows, LANES), lambda s: (s, 0, 0)),
        scratch_shapes=[
            pltpu.VMEM((2 * CHUNK * rows, full), jnp.bfloat16),
            pltpu.VMEM((full, LANES), jnp.bfloat16),
            pltpu.VMEM((CHUNK * out_rows, CHUNK * rows), jnp.bfloat16),
            pltpu.VMEM((2 * CHUNK, out_rows, LANES), jnp.float32),
        ],
        compiler_params=pltpu.CompilerParams(vmem_limit_bytes=48 * 2**20),
        name="work_pairs",
    )(jnp.asarray(FIRST), jnp.asarray(SECOND), win_rows, win_cols, held)


def collect_kernel(groups, result, parts, send, recv, up_send, up_recv, local):
    date = lax.axis_index("date")
    group, member = date // GROUP, date % GROUP
    base = group * GROUP
    has_before, has_after = group > 0, group < groups - 1
    late = [k for k in range(GROUP) if UPS[k]]

    def is_late(who):
        return who >= late[0]

    barrier = pltpu.get_barrier_semaphore()
    for k in (1, 2, 3):
        pl.semaphore_signal(
            barrier, inc=1, device_id={"date": base + other_member(member, k)}, device_id_type=MESH
        )

    @pl.when(has_before)
    def _():
        for k in late:
            pl.semaphore_signal(
                barrier, inc=1, device_id={"date": base - GROUP + k}, device_id_type=MESH
            )

    @pl.when(jnp.logical_and(has_after, is_late(member)))
    def _():
        for k in range(GROUP):
            pl.semaphore_signal(
                barrier, inc=1, device_id={"date": base + GROUP + k}, device_id_type=MESH
            )

    from_after = jnp.logical_and(has_after, is_late(member)).astype(jnp.int32)
    peers = GROUP - 1 + has_before.astype(jnp.int32) * len(late) + from_after * GROUP
    pl.semaphore_wait(barrier, peers)

    def near(source, target):
        return pltpu.make_async_remote_copy(
            src_ref=result.at[pl.ds(STARTS[target], COUNTS[target])],
            dst_ref=parts.at[source, pl.ds(0, COUNTS[target])],
            send_sem=send.at[target],
            recv_sem=recv.at[source],
            device_id={"date": base + target},
            device_id_type=MESH,
        )

    def up(source, target):
        return pltpu.make_async_remote_copy(
            src_ref=result.at[pl.ds(UP_STARTS[target], UPS[target])],
            dst_ref=parts.at[source, pl.ds(COUNTS[target], UPS[target])],
            send_sem=up_send.at[target],
            recv_sem=up_recv.at[source],
            device_id={"date": base - GROUP + target},
            device_id_type=MESH,
        )

    def keep(target):
        return pltpu.make_async_copy(
            result.at[pl.ds(STARTS[target], COUNTS[target])],
            parts.at[target, pl.ds(0, COUNTS[target])],
            local.at[0],
        )

    @pl.when(has_before)
    def _():
        for target in late:
            up(member, target).start()

    for target in range(GROUP):

        @pl.when(member != target)
        def _():
            near(member, target).start()

        @pl.when(member == target)
        def _():
            keep(target).start()

    for target in range(GROUP):

        @pl.when(member != target)
        def _():
            near(member, target).wait_send()

        @pl.when(member == target)
        def _():
            keep(target).wait()
            for source in range(GROUP):
                if source != target:
                    near(source, target).wait_recv()

    @pl.when(has_before)
    def _():
        for target in late:
            up(member, target).wait_send()

    for target in late:

        @pl.when(jnp.logical_and(has_after, member == target))
        def _():
            for source in range(GROUP):
                up(source, target).wait_recv()


def collect(result, groups):
    return pl.pallas_call(
        functools.partial(collect_kernel, groups),
        out_shape=jax.ShapeDtypeStruct((GROUP, OWN * SPAN, *result.shape[1:]), result.dtype),
        in_specs=[pl.BlockSpec(memory_space=pl.ANY)],
        out_specs=pl.BlockSpec(memory_space=pl.ANY),
        scratch_shapes=[pltpu.SemaphoreType.DMA((GROUP,))] * 4 + [pltpu.SemaphoreType.DMA((1,))],
        compiler_params=pltpu.CompilerParams(collective_id=1, has_side_effects=True),
        name="collect",
    )(result)


def slots_kernel(count, pair_list, place, parts, out):
    date = lax.axis_index("date")
    member = date % GROUP
    half = LANES // 2
    left = lax.broadcasted_iota(jnp.int32, (parts.shape[2], LANES), 1) < half

    def one_slot(s, carry):
        i = pair_list[s, 0]
        alive = i >= 0
        at = (i - date * OWN) * SPAN + pair_list[s, 1] - i - 1
        at = jnp.clip(jnp.where(alive, at, 0), 0, OWN * SPAN - 1)
        at = place[member, at]
        for n in range(GROUP // 2):
            a = parts[2 * n, at]
            b = parts[2 * n + 1, at]
            re = jnp.where(left, a, pltpu.roll(b, half, 1))
            im = jnp.where(left, pltpu.roll(a, half, 1), b)
            out[0, s, :, n * LANES : (n + 1) * LANES] = jnp.where(alive, re, 0.0)
            out[1, s, :, n * LANES : (n + 1) * LANES] = jnp.where(alive, im, 0.0)
        return carry

    lax.fori_loop(0, count, one_slot, 0)


def to_slots(pair_list, parts):
    count = pair_list.shape[0]
    smem = pl.BlockSpec(memory_space=pltpu.SMEM)
    vmem = pl.BlockSpec(memory_space=pltpu.VMEM)
    return pl.pallas_call(
        functools.partial(slots_kernel, count),
        out_shape=jax.ShapeDtypeStruct(
            (2, count, parts.shape[2], GROUP * LANES // 2), jnp.float32
        ),
        in_specs=[smem, smem, vmem],
        out_specs=vmem,
        compiler_params=pltpu.CompilerParams(vmem_limit_bytes=16 * 2**20),
        name="to_slots",
    )(pair_list, jnp.asarray(PLACE), parts)


def rims(acq):
    cols = acq.shape[3]
    width = cols // GROUP
    tile = lax.axis_index("tile")
    outgoing = jnp.where(tile == 0, acq[..., cols - HALF :], acq[..., :HALF])
    incoming = lax.ppermute(outgoing, "tile", [(0, 1), (1, 0)])
    nothing = jnp.zeros_like(incoming)
    lower = jnp.where(tile == 1, incoming, nothing)
    upper = jnp.where(tile == 0, incoming, nothing)
    pad = jnp.zeros((*acq.shape[:3], LANES - 2 * HALF), acq.dtype)
    pieces = []
    for k in range(GROUP):
        left = lower if k == 0 else acq[..., k * width - HALF : k * width]
        right = upper if k == GROUP - 1 else acq[..., (k + 1) * width : (k + 1) * width + HALF]
        pieces.append(jnp.concatenate((left, right, pad), axis=3))
    return jnp.stack(pieces)


def shards(groups, acquisitions, pair_list, win_rows, win_cols):
    held = spread(acquisitions, rims(acquisitions), groups)
    result = work_pairs(held, win_rows, win_cols)
    parts = collect(result, groups)
    return to_slots(pair_list, parts)


def solution(mesh):
    return jax.shard_map(
        functools.partial(shards, mesh.shape["date"] // GROUP),
        mesh=mesh,
        in_specs=(P(None, "date", "grp", "tile"), P("date", None), P(), P()),
        out_specs=P(None, "date", "grp", "tile"),
        check_vma=False,
    )
```

```python
import functools

import jax
import jax.numpy as jnp
import numpy as np
from jax import lax
from jax.experimental import pallas as pl
from jax.experimental.pallas import tpu as pltpu
from jax.sharding import PartitionSpec as P

SPAN = 15
STRIDE_R = 4
STRIDE_C = 16
EPS = 1e-06

GROUP = 4
OWN = 4
LOCAL = GROUP * OWN
DOWN = 8
UP_FROM = DOWN + 1
UP = LOCAL - UP_FROM
HELD = LOCAL + DOWN + UP
HALF = STRIDE_C // 2
LANES = 128
CHUNK = 16
MESH = pl.DeviceIdType.MESH


def pair_plan():
    first, second, counts, ups = [], [], [], []
    place = np.zeros((GROUP, OWN * SPAN), np.int32)
    near = [min(SPAN, LOCAL + DOWN - 1 - i) for i in range(LOCAL)]
    for member in range(GROUP):
        at = 0
        for step in range(OWN):
            i = member * OWN + step
            for d in range(near[i]):
                first.append(i)
                second.append(i + 1 + d)
                place[member, step * SPAN + d] = at
                at += 1
        counts.append(at)
        for step in range(OWN):
            i = member * OWN + step
            for d in range(near[i], SPAN):
                place[member, step * SPAN + d] = at
                at += 1
        ups.append(at - counts[-1])
    for member in range(GROUP):
        for step in range(OWN):
            i = member * OWN + step
            for d in range(near[i], SPAN):
                first.append(LOCAL + DOWN + i - UP_FROM)
                second.append(i + 1 + d - LOCAL)
    return np.array(first, np.int32), np.array(second, np.int32), counts, ups, place


FIRST, SECOND, COUNTS, UPS, PLACE = pair_plan()
TOTAL = len(FIRST)
STARTS = [sum(COUNTS[:k]) for k in range(GROUP)]
UP_STARTS = [sum(COUNTS) + sum(UPS[:k]) for k in range(GROUP)]


def other_member(member, k):
    if k == 1:
        return member + 1 - 2 * (member % 2)
    if k == 2:
        return member + 2 - 4 * (member // 2)
    return GROUP - 1 - member


def spread_kernel(groups, width, acq, rim, held, send, recv, far_send, far_recv, local):
    date = lax.axis_index("date")
    group, member = date // GROUP, date % GROUP
    base = group * GROUP
    has_before, has_after = group > 0, group < groups - 1

    barrier = pltpu.get_barrier_semaphore()
    for k in (1, 2, 3):
        pl.semaphore_signal(
            barrier, inc=1, device_id={"date": base + other_member(member, k)}, device_id_type=MESH
        )

    @pl.when(has_before)
    def _():
        pl.semaphore_signal(barrier, inc=1, device_id={"date": date - GROUP}, device_id_type=MESH)

    @pl.when(has_after)
    def _():
        pl.semaphore_signal(barrier, inc=1, device_id={"date": date + GROUP}, device_id_type=MESH)

    peers = GROUP - 1 + has_before.astype(jnp.int32) + has_after.astype(jnp.int32)
    pl.semaphore_wait(barrier, peers)

    def body_of(who):
        return acq.at[:, :, :, pl.ds(pl.multiple_of(who * width, width), width)]

    def rim_of(who):
        return rim.at[who]

    def slot(start, count):
        part = held.at[:, pl.ds(start, count)]
        return part.at[:, :, :, pl.ds(0, width)], part.at[:, :, :, pl.ds(width, LANES)]

    near = []
    for k in (1, 2, 3):
        who = other_member(member, k)
        main, side = slot(member * OWN, OWN)
        pair = [
            pltpu.make_async_remote_copy(
                src_ref=src,
                dst_ref=dst,
                send_sem=send.at[k, n],
                recv_sem=recv.at[k, n],
                device_id={"date": base + who},
                device_id_type=MESH,
            )
            for n, (src, dst) in enumerate(((body_of(who), main), (rim_of(who), side)))
        ]
        for copy in pair:
            copy.start()
        near.append(pair)
    main, side = slot(member * OWN, OWN)
    mine = [
        pltpu.make_async_copy(body_of(member), main, local.at[0]),
        pltpu.make_async_copy(rim_of(member), side, local.at[1]),
    ]

    onward = [
        (0, OWN, LOCAL, -1),
        (OWN, OWN, LOCAL + OWN, -1),
        (UP_FROM, 3 * OWN - UP_FROM, LOCAL + DOWN, 1),
        (3 * OWN, OWN, LOCAL + DOWN + 3 * OWN - UP_FROM, 1),
    ]

    def far(source):
        start, count, place, step = onward[source]
        return [
            pltpu.make_async_remote_copy(
                src_ref=src,
                dst_ref=dst,
                send_sem=far_send.at[source, n],
                recv_sem=far_recv.at[source, n],
                device_id={"date": date + step * GROUP},
                device_id_type=MESH,
            )
            for n, (src, dst) in enumerate(zip(slot(start, count), slot(place, count)))
        ]

    def far_mine(source):
        start, count, place, step = onward[source]
        skip = start - source * OWN
        main, side = slot(place, count)
        return [
            pltpu.make_async_remote_copy(
                src_ref=src.at[:, pl.ds(skip, count)],
                dst_ref=dst,
                send_sem=far_send.at[source, n],
                recv_sem=far_recv.at[source, n],
                device_id={"date": date + step * GROUP},
                device_id_type=MESH,
            )
            for n, (src, dst) in enumerate(((body_of(source), main), (rim_of(source), side)))
        ]

    def pass_on(who):
        for source in range(GROUP):
            exists = has_before if onward[source][3] < 0 else has_after

            @pl.when(jnp.logical_and(who == source, exists))
            def _():
                for copy in far(source):
                    copy.start()

    for source in range(GROUP):
        exists = has_before if onward[source][3] < 0 else has_after

        @pl.when(jnp.logical_and(member == source, exists))
        def _():
            for copy in far_mine(source):
                copy.start()

    for copy in mine:
        copy.start()
    for k in (1, 2, 3):
        for copy in near[k - 1]:
            copy.wait_recv()
        pass_on(other_member(member, k))
    for copy in mine:
        copy.wait()
    for pair in near:
        for copy in pair:
            copy.wait_send()

    for source in range(GROUP):
        start, count, place, step = onward[source]
        sends = has_before if step < 0 else has_after
        gets = has_after if step < 0 else has_before

        @pl.when(sends)
        def _():
            for copy in far(source):
                copy.wait_send()

        @pl.when(gets)
        def _():
            for copy in far(source):
                copy.wait_recv()


def spread(acq, rim, groups):
    width = acq.shape[3] // GROUP
    return pl.pallas_call(
        functools.partial(spread_kernel, groups, width),
        out_shape=jax.ShapeDtypeStruct((2, HELD, acq.shape[2], width + LANES), acq.dtype),
        in_specs=[pl.BlockSpec(memory_space=pl.ANY)] * 2,
        out_specs=pl.BlockSpec(memory_space=pl.ANY),
        scratch_shapes=[
            pltpu.SemaphoreType.DMA((GROUP, 2)),
            pltpu.SemaphoreType.DMA((GROUP, 2)),
            pltpu.SemaphoreType.DMA((GROUP, 2)),
            pltpu.SemaphoreType.DMA((GROUP, 2)),
            pltpu.SemaphoreType.DMA((2,)),
        ],
        compiler_params=pltpu.CompilerParams(collective_id=0, has_side_effects=True),
        name="spread",
    )(acq, rim)


def split_dot(taps, values):
    high = values.astype(jnp.bfloat16)
    low = (values - high.astype(jnp.float32)).astype(jnp.bfloat16)
    return jnp.dot(taps, high, preferred_element_type=jnp.float32) + jnp.dot(
        taps, low, preferred_element_type=jnp.float32
    )


def pairs_kernel(
    rows,
    width,
    groups,
    first,
    second,
    win_rows,
    win_cols,
    held,
    result,
    wide,
    product,
    col_taps,
    row_taps,
    power,
):
    out_rows = rows // STRIDE_R
    out_cols = width // STRIDE_C
    full = width + LANES
    step = pl.program_id(0)
    cuts = [(r, c) for r in range(0, rows, 16) for c in range(0, full, 384)]
    group = lax.axis_index("date") // GROUP

    def present(d):
        missing = jnp.logical_or(
            jnp.logical_and(group == 0, d >= LOCAL + DOWN),
            jnp.logical_and(group == groups - 1, jnp.logical_and(d >= LOCAL, d < LOCAL + DOWN)),
        )
        return jnp.where(missing, 0, d)

    @pl.when(step == 0)
    def _():
        lane = lax.broadcasted_iota(jnp.int32, (full, LANES), 0)
        out = lax.broadcasted_iota(jnp.int32, (full, LANES), 1) % out_cols
        column = jnp.where(
            lane < width, lane, jnp.where(lane < width + HALF, lane - width - HALF, lane - HALF)
        )
        near = jnp.abs(2 * column + 1 - (2 * out + 1) * STRIDE_C) <= win_cols[0]
        near = jnp.logical_and(near, lane < width + 2 * HALF)
        col_taps[...] = jnp.where(near, 1.0, 0.0).astype(jnp.bfloat16)

        shape = (CHUNK * out_rows, CHUNK * rows)
        at = lax.broadcasted_iota(jnp.int32, shape, 0)
        row = lax.broadcasted_iota(jnp.int32, shape, 1)
        window = jnp.zeros(shape, jnp.int32)
        for o in range(out_rows):
            window = jnp.where(at % out_rows == o, win_rows[o], window)
        inside = jnp.abs(2 * (row % rows) + 1 - (2 * (at % out_rows) + 1) * STRIDE_R) <= window
        inside = jnp.logical_and(inside, at // out_rows == row // rows)
        row_taps[...] = jnp.where(inside, 1.0, 0.0).astype(jnp.bfloat16)

        def one_date(d, carry):
            for r, c in cuts:
                re = held[0, present(d), r : r + 16, c : c + 384].astype(jnp.float32)
                im = held[1, present(d), r : r + 16, c : c + 384].astype(jnp.float32)
                wide[0, d, r : r + 16, c : c + 384] = re
                wide[1, d, r : r + 16, c : c + 384] = im
                at = pl.multiple_of(d * rows + r, 16)
                product[pl.ds(at, 16), c : c + 384] = (re * re + im * im).astype(jnp.bfloat16)
            return carry

        lax.fori_loop(0, HELD, one_date, 0)
        product[HELD * rows :] = jnp.zeros((2 * CHUNK * rows - HELD * rows, full), jnp.bfloat16)
        across = jnp.dot(product[...], col_taps[...], preferred_element_type=jnp.float32)
        half = CHUNK * rows
        for n in range(2):
            looked = split_dot(row_taps[...], across[n * half : (n + 1) * half])
            power[n * CHUNK : (n + 1) * CHUNK] = looked.reshape(CHUNK, out_rows, LANES)

    def one_pair(p, carry):
        i = first[step * CHUNK + p]
        j = second[step * CHUNK + p]
        for r, c in cuts:
            re_i = wide[0, i, r : r + 16, c : c + 384]
            im_i = wide[1, i, r : r + 16, c : c + 384]
            re_j = wide[0, j, r : r + 16, c : c + 384]
            im_j = wide[1, j, r : r + 16, c : c + 384]
            at = pl.multiple_of(p * 2 * rows + r, 16)
            product[pl.ds(at, 16), c : c + 384] = (re_i * re_j + im_i * im_j).astype(jnp.bfloat16)
            at = pl.multiple_of(p * 2 * rows + rows + r, 16)
            product[pl.ds(at, 16), c : c + 384] = (im_i * re_j - re_i * im_j).astype(jnp.bfloat16)
        return carry

    lax.fori_loop(0, CHUNK, one_pair, 0)
    across = jnp.dot(product[...], col_taps[...], preferred_element_type=jnp.float32)
    across = across.reshape(CHUNK, 2, rows, LANES)
    lane = lax.broadcasted_iota(jnp.int32, (CHUNK, rows, LANES), 2)
    both = jnp.where(lane < out_cols, across[:, 0], across[:, 1]).reshape(CHUNK * rows, LANES)
    looked = split_dot(row_taps[...], both).reshape(CHUNK, out_rows, LANES)
    for p in range(CHUNK):
        i = first[step * CHUNK + p]
        j = second[step * CHUNK + p]
        result[p] = looked[p] * lax.rsqrt(power[i] * power[j] + EPS)


def work_pairs(held, win_rows, win_cols, groups):
    rows, full = held.shape[2:]
    width = full - LANES
    out_rows = rows // STRIDE_R
    smem = pl.BlockSpec(memory_space=pltpu.SMEM)
    return pl.pallas_call(
        functools.partial(pairs_kernel, rows, width, groups),
        grid=(TOTAL // CHUNK,),
        out_shape=jax.ShapeDtypeStruct((TOTAL, out_rows, LANES), jnp.float32),
        in_specs=[smem, smem, smem, smem, pl.BlockSpec(held.shape, lambda s: (0, 0, 0, 0))],
        out_specs=pl.BlockSpec((CHUNK, out_rows, LANES), lambda s: (s, 0, 0)),
        scratch_shapes=[
            pltpu.VMEM(held.shape, jnp.float32),
            pltpu.VMEM((2 * CHUNK * rows, full), jnp.bfloat16),
            pltpu.VMEM((full, LANES), jnp.bfloat16),
            pltpu.VMEM((CHUNK * out_rows, CHUNK * rows), jnp.bfloat16),
            pltpu.VMEM((2 * CHUNK, out_rows, LANES), jnp.float32),
        ],
        compiler_params=pltpu.CompilerParams(vmem_limit_bytes=48 * 2**20),
        name="work_pairs",
    )(jnp.asarray(FIRST), jnp.asarray(SECOND), win_rows, win_cols, held)


def collect_kernel(groups, result, parts, send, recv, up_send, up_recv, local):
    date = lax.axis_index("date")
    group, member = date // GROUP, date % GROUP
    base = group * GROUP
    has_before, has_after = group > 0, group < groups - 1
    late = [k for k in range(GROUP) if UPS[k]]

    def is_late(who):
        return who >= late[0]

    barrier = pltpu.get_barrier_semaphore()
    for k in (1, 2, 3):
        pl.semaphore_signal(
            barrier, inc=1, device_id={"date": base + other_member(member, k)}, device_id_type=MESH
        )

    @pl.when(has_before)
    def _():
        for k in late:
            pl.semaphore_signal(
                barrier, inc=1, device_id={"date": base - GROUP + k}, device_id_type=MESH
            )

    @pl.when(jnp.logical_and(has_after, is_late(member)))
    def _():
        for k in range(GROUP):
            pl.semaphore_signal(
                barrier, inc=1, device_id={"date": base + GROUP + k}, device_id_type=MESH
            )

    from_after = jnp.logical_and(has_after, is_late(member)).astype(jnp.int32)
    peers = GROUP - 1 + has_before.astype(jnp.int32) * len(late) + from_after * GROUP
    pl.semaphore_wait(barrier, peers)

    def near(source, target):
        return pltpu.make_async_remote_copy(
            src_ref=result.at[pl.ds(STARTS[target], COUNTS[target])],
            dst_ref=parts.at[source, pl.ds(0, COUNTS[target])],
            send_sem=send.at[target],
            recv_sem=recv.at[source],
            device_id={"date": base + target},
            device_id_type=MESH,
        )

    def up(source, target):
        return pltpu.make_async_remote_copy(
            src_ref=result.at[pl.ds(UP_STARTS[target], UPS[target])],
            dst_ref=parts.at[source, pl.ds(COUNTS[target], UPS[target])],
            send_sem=up_send.at[target],
            recv_sem=up_recv.at[source],
            device_id={"date": base - GROUP + target},
            device_id_type=MESH,
        )

    def keep(target):
        return pltpu.make_async_copy(
            result.at[pl.ds(STARTS[target], COUNTS[target])],
            parts.at[target, pl.ds(0, COUNTS[target])],
            local.at[0],
        )

    @pl.when(has_before)
    def _():
        for target in late:
            up(member, target).start()

    for target in range(GROUP):

        @pl.when(member != target)
        def _():
            near(member, target).start()

        @pl.when(member == target)
        def _():
            keep(target).start()

    for target in range(GROUP):

        @pl.when(member != target)
        def _():
            near(member, target).wait_send()

        @pl.when(member == target)
        def _():
            keep(target).wait()
            for source in range(GROUP):
                if source != target:
                    near(source, target).wait_recv()

    @pl.when(has_before)
    def _():
        for target in late:
            up(member, target).wait_send()

    for target in late:

        @pl.when(jnp.logical_and(has_after, member == target))
        def _():
            for source in range(GROUP):
                up(source, target).wait_recv()


def collect(result, groups):
    return pl.pallas_call(
        functools.partial(collect_kernel, groups),
        out_shape=jax.ShapeDtypeStruct((GROUP, OWN * SPAN, *result.shape[1:]), result.dtype),
        in_specs=[pl.BlockSpec(memory_space=pl.ANY)],
        out_specs=pl.BlockSpec(memory_space=pl.ANY),
        scratch_shapes=[pltpu.SemaphoreType.DMA((GROUP,))] * 4 + [pltpu.SemaphoreType.DMA((1,))],
        compiler_params=pltpu.CompilerParams(collective_id=1, has_side_effects=True),
        name="collect",
    )(result)


def slots_kernel(count, pair_list, place, parts, out):
    date = lax.axis_index("date")
    member = date % GROUP
    half = LANES // 2
    left = lax.broadcasted_iota(jnp.int32, (parts.shape[2], LANES), 1) < half

    def one_slot(s, carry):
        i = pair_list[s, 0]
        alive = i >= 0
        at = (i - date * OWN) * SPAN + pair_list[s, 1] - i - 1
        at = jnp.clip(jnp.where(alive, at, 0), 0, OWN * SPAN - 1)
        at = place[member, at]
        for n in range(GROUP // 2):
            a = parts[2 * n, at]
            b = parts[2 * n + 1, at]
            re = jnp.where(left, a, pltpu.roll(b, half, 1))
            im = jnp.where(left, pltpu.roll(a, half, 1), b)
            out[0, s, :, n * LANES : (n + 1) * LANES] = jnp.where(alive, re, 0.0)
            out[1, s, :, n * LANES : (n + 1) * LANES] = jnp.where(alive, im, 0.0)
        return carry

    lax.fori_loop(0, count, one_slot, 0)


def to_slots(pair_list, parts):
    count = pair_list.shape[0]
    smem = pl.BlockSpec(memory_space=pltpu.SMEM)
    vmem = pl.BlockSpec(memory_space=pltpu.VMEM)
    return pl.pallas_call(
        functools.partial(slots_kernel, count),
        out_shape=jax.ShapeDtypeStruct(
            (2, count, parts.shape[2], GROUP * LANES // 2), jnp.float32
        ),
        in_specs=[smem, smem, vmem],
        out_specs=vmem,
        compiler_params=pltpu.CompilerParams(vmem_limit_bytes=16 * 2**20),
        name="to_slots",
    )(pair_list, jnp.asarray(PLACE), parts)


def rims(acq):
    cols = acq.shape[3]
    width = cols // GROUP
    tile = lax.axis_index("tile")
    outgoing = jnp.where(tile == 0, acq[..., cols - HALF :], acq[..., :HALF])
    incoming = lax.ppermute(outgoing, "tile", [(0, 1), (1, 0)])
    nothing = jnp.zeros_like(incoming)
    lower = jnp.where(tile == 1, incoming, nothing)
    upper = jnp.where(tile == 0, incoming, nothing)
    pad = jnp.zeros((*acq.shape[:3], LANES - 2 * HALF), acq.dtype)
    pieces = []
    for k in range(GROUP):
        left = lower if k == 0 else acq[..., k * width - HALF : k * width]
        right = upper if k == GROUP - 1 else acq[..., (k + 1) * width : (k + 1) * width + HALF]
        pieces.append(jnp.concatenate((left, right, pad), axis=3))
    return jnp.stack(pieces)


def shards(groups, acquisitions, pair_list, win_rows, win_cols):
    held = spread(acquisitions, rims(acquisitions), groups)
    result = work_pairs(held, win_rows, win_cols, groups)
    parts = collect(result, groups)
    return to_slots(pair_list, parts)


def solution(mesh):
    return jax.shard_map(
        functools.partial(shards, mesh.shape["date"] // GROUP),
        mesh=mesh,
        in_specs=(P(None, "date", "grp", "tile"), P("date", None), P(), P()),
        out_specs=P(None, "date", "grp", "tile"),
        check_vma=False,
    )
```

```python
import functools

import jax
import jax.numpy as jnp
from jax import lax
from jax.experimental import pallas as pl
from jax.experimental.pallas import tpu as pltpu
from jax.sharding import PartitionSpec as P

SPAN = 15
STRIDE_R = 4
STRIDE_C = 16
EPS = 1e-06

GROUP = 4
OWN = 4
LOCAL = GROUP * OWN
DOWN = 8
UP_FROM = DOWN + 1
UP = LOCAL - UP_FROM
HELD = LOCAL + DOWN + UP
HALF = STRIDE_C // 2
LANES = 128
CHUNK = 24
MESH = pl.DeviceIdType.MESH


INSIDE = LOCAL * (LOCAL - 1) // 2
RECT = (LOCAL - DOWN) * DOWN
FOLD = DOWN * (DOWN - 1) // 2
UPS = (0, 0, 6, 22)
OUTBOX = LOCAL * SPAN


def other_member(member, k):
    if k == 1:
        return member + 1 - 2 * (member % 2)
    if k == 2:
        return member + 2 - 4 * (member // 2)
    return GROUP - 1 - member


def inside_pair(f):
    x = lax.rem(f, LOCAL)
    y = x + lax.div(f, LOCAL) + 1
    turn = lax.div(y, LOCAL)
    i = x * (1 - turn) + (y - LOCAL) * turn
    j = y * (1 - turn) + x * turn
    return i, j, i * SPAN + j - i - 1


def cross_pair(f):
    beyond = lax.div(f, RECT)
    up = lax.div(f, RECT + FOLD)
    e = (f - RECT - FOLD * up) * beyond
    row = lax.div(e, DOWN - 1)
    col = lax.rem(e, DOWN - 1)
    turn = lax.div(col + row, DOWN - 1)
    size = (DOWN - 1 - row) * (1 - turn) + row * turn
    inner = col - (DOWN - 1 - row) * turn
    i = (1 - beyond) * (DOWN + lax.div(f, DOWN)) + (beyond - up) * size
    j = (1 - beyond) * lax.rem(f, DOWN) + (beyond - up) * inner + LOCAL
    i = (1 - up) * i + up * (LOCAL + DOWN + size - 1)
    j = (1 - up) * j + up * (DOWN + inner)
    near = i * SPAN + j - i - 1
    far = OUTBOX + lax.div(size * (size - 1), 2) + inner
    return i, j, (1 - up) * near + up * far


def split_dot(taps, values):
    high = values.astype(jnp.bfloat16)
    low = (values - high.astype(jnp.float32)).astype(jnp.bfloat16)
    return jnp.dot(taps, high, preferred_element_type=jnp.float32) + jnp.dot(
        taps, low, preferred_element_type=jnp.float32
    )


def strip_kernel(
    groups,
    rows,
    width,
    win_rows,
    win_cols,
    acq,
    rim,
    parts,
    held,
    wide,
    product,
    col_taps,
    row_taps,
    power,
    looked,
    outbox,
    send,
    recv,
    far_send,
    far_recv,
    local,
    back_send,
    back_recv,
    up_send,
    up_recv,
):
    out_rows = rows // STRIDE_R
    out_cols = width // STRIDE_C
    full = width + LANES
    cuts = [(r, c) for r in range(0, rows, 16) for c in range(0, full, 384)]
    date = lax.axis_index("date")
    group, member = date // GROUP, date % GROUP
    base = group * GROUP
    has_before, has_after = group > 0, group < groups - 1
    is_late = member >= 2

    def greet(where):
        pl.semaphore_signal(
            pltpu.get_barrier_semaphore(),
            inc=1,
            device_id={"date": where},
            device_id_type=MESH,
        )

    for k in (1, 2, 3):
        greet(base + other_member(member, k))

    @pl.when(has_before)
    def _():
        greet(date - GROUP)
        for k in (2, 3):

            @pl.when(member != k)
            def _():
                greet(base - GROUP + k)

    @pl.when(has_after)
    def _():
        greet(date + GROUP)

        @pl.when(is_late)
        def _():
            for k in (1, 2, 3):
                greet(base + GROUP + other_member(member, k))

    late = member // 2
    peers = GROUP - 1 + has_before.astype(jnp.int32) * (3 - late)
    peers = peers + has_after.astype(jnp.int32) * (1 + 3 * late)
    pl.semaphore_wait(pltpu.get_barrier_semaphore(), peers)

    def body_of(who):
        return acq.at[:, :, :, pl.ds(pl.multiple_of(who * width, width), width)]

    def rim_of(who):
        return rim.at[who]

    def slot(start, count):
        part = held.at[:, pl.ds(start, count)]
        return part.at[:, :, :, pl.ds(0, width)], part.at[:, :, :, pl.ds(width, LANES)]

    def remote(src, dst, send_sem, recv_sem, where):
        return pltpu.make_async_remote_copy(
            src_ref=src,
            dst_ref=dst,
            send_sem=send_sem,
            recv_sem=recv_sem,
            device_id={"date": where},
            device_id_type=MESH,
        )

    onward = [
        (0, OWN, LOCAL, -1),
        (OWN, OWN, LOCAL + OWN, -1),
        (UP_FROM, 3 * OWN - UP_FROM, LOCAL + DOWN, 1),
        (3 * OWN, OWN, LOCAL + DOWN + 3 * OWN - UP_FROM, 1),
    ]

    def far(source, mine):
        start, count, place, step = onward[source]
        if mine:
            skip = start - source * OWN
            srcs = [ref.at[:, pl.ds(skip, count)] for ref in (body_of(source), rim_of(source))]
        else:
            srcs = slot(start, count)
        return [
            remote(
                src, dst, far_send.at[source, n], far_recv.at[source, n], date + step * GROUP
            )
            for n, (src, dst) in enumerate(zip(srcs, slot(place, count)))
        ]

    def pass_on(who, mine):
        for source in range(GROUP):
            exists = has_before if onward[source][3] < 0 else has_after

            @pl.when(jnp.logical_and(who == source, exists))
            def _():
                for copy in far(source, mine):
                    copy.start()

    near = []
    for k in (1, 2, 3):
        who = other_member(member, k)
        pair = [
            remote(src, dst, send.at[k, n], recv.at[k, n], base + who)
            for n, (src, dst) in enumerate(
                zip((body_of(who), rim_of(who)), slot(member * OWN, OWN))
            )
        ]
        for copy in pair:
            copy.start()
        near.append(pair)
    pass_on(member, True)
    main, side = slot(member * OWN, OWN)
    mine = [
        pltpu.make_async_copy(body_of(member), main, local.at[0]),
        pltpu.make_async_copy(rim_of(member), side, local.at[1]),
    ]
    for copy in mine:
        copy.start()

    lane = lax.broadcasted_iota(jnp.int32, (full, LANES), 0)
    out = lax.broadcasted_iota(jnp.int32, (full, LANES), 1) % out_cols
    column = jnp.where(
        lane < width, lane, jnp.where(lane < width + HALF, lane - width - HALF, lane - HALF)
    )
    beside = jnp.abs(2 * column + 1 - (2 * out + 1) * STRIDE_C) <= win_cols[0]
    beside = jnp.logical_and(beside, lane < width + 2 * HALF)
    col_taps[...] = jnp.where(beside, 1.0, 0.0).astype(jnp.bfloat16)
    shape = (CHUNK * out_rows, CHUNK * rows)
    at = lax.broadcasted_iota(jnp.int32, shape, 0)
    row = lax.broadcasted_iota(jnp.int32, shape, 1)
    window = jnp.zeros(shape, jnp.int32)
    for o in range(out_rows):
        window = jnp.where(at % out_rows == o, win_rows[o], window)
    inside = jnp.abs(2 * (row % rows) + 1 - (2 * (at % out_rows) + 1) * STRIDE_R) <= window
    inside = jnp.logical_and(inside, at // out_rows == row // rows)
    row_taps[...] = jnp.where(inside, 1.0, 0.0).astype(jnp.bfloat16)

    def widen(start, count, shift):
        def one_date(n, carry):
            d = start + n
            for r, c in cuts:
                re = held[0, d, r : r + 16, c : c + 384].astype(jnp.float32)
                im = held[1, d, r : r + 16, c : c + 384].astype(jnp.float32)
                wide[0, d, r : r + 16, c : c + 384] = re
                wide[1, d, r : r + 16, c : c + 384] = im
                to = pl.multiple_of((d - shift) * rows + r, 16)
                product[pl.ds(to, 16), c : c + 384] = (re * re + im * im).astype(jnp.bfloat16)
            return carry

        lax.fori_loop(0, count, one_date, 0)

    def blank(start, count, shift):
        def one_date(n, carry):
            d = start + n
            for part in range(2):
                wide[part, d] = jnp.zeros((rows, full), jnp.float32)
            to = pl.multiple_of((d - shift) * rows, 16)
            product[pl.ds(to, rows), :] = jnp.zeros((rows, full), jnp.bfloat16)
            return carry

        lax.fori_loop(0, count, one_date, 0)

    def look_power(start):
        across = jnp.dot(
            product[: LOCAL * rows], col_taps[...], preferred_element_type=jnp.float32
        )
        taps = row_taps[: LOCAL * out_rows, : LOCAL * rows]
        power[start : start + LOCAL] = split_dot(taps, across).reshape(LOCAL, out_rows, LANES)

    def work(total, pair_of):
        def one_chunk(chunk, carry):
            def one_pair(p, carry):
                i, j, _ = pair_of(chunk * CHUNK + p)
                for r, c in cuts:
                    re_i = wide[0, i, r : r + 16, c : c + 384]
                    im_i = wide[1, i, r : r + 16, c : c + 384]
                    re_j = wide[0, j, r : r + 16, c : c + 384]
                    im_j = wide[1, j, r : r + 16, c : c + 384]
                    re = (re_i * re_j + im_i * im_j).astype(jnp.bfloat16)
                    im = (im_i * re_j - re_i * im_j).astype(jnp.bfloat16)
                    product[pl.ds(pl.multiple_of(p * 2 * rows + r, 16), 16), c : c + 384] = re
                    at = pl.multiple_of(p * 2 * rows + rows + r, 16)
                    product[pl.ds(at, 16), c : c + 384] = im
                return carry

            lax.fori_loop(0, CHUNK, one_pair, 0)
            across = jnp.dot(product[...], col_taps[...], preferred_element_type=jnp.float32)
            across = across.reshape(CHUNK, 2, rows, LANES)
            left = lax.broadcasted_iota(jnp.int32, (CHUNK, rows, LANES), 2) < out_cols
            both = jnp.where(left, across[:, 0], across[:, 1]).reshape(CHUNK * rows, LANES)
            looked[...] = split_dot(row_taps[...], both).reshape(CHUNK, out_rows, LANES)

            def finish(p, carry):
                i, j, to = pair_of(chunk * CHUNK + p)
                outbox[to] = looked[p] * lax.rsqrt(power[i] * power[j] + EPS)
                return carry

            lax.fori_loop(0, CHUNK, finish, 0)
            return carry

        lax.fori_loop(0, total // CHUNK, one_chunk, 0)

    def back(source, target, step, part):
        i = target * OWN + step
        if part == 0:
            start, count = 0, SPAN - i
        else:
            start, count = SPAN - i, min(i, DOWN)
        src = outbox.at[pl.ds(i * SPAN + start, count)]
        dst = parts.at[source, pl.ds(step * SPAN + start, count)]
        return src, dst, count

    def back_copies(source, target, part):
        copies = []
        for step in range(OWN):
            src, dst, count = back(source, target, step, part)
            if count:
                copies.append(
                    remote(
                        src,
                        dst,
                        back_send.at[part, target, step],
                        back_recv.at[part, source, step],
                        base + target,
                    )
                )
        return copies

    def kept_copies(target, part):
        copies = []
        for step in range(OWN):
            src, dst, count = back(target, target, step, part)
            if count:
                sem = back_send.at[part, target, step]
                copies.append(pltpu.make_async_copy(src, dst, sem))
        return copies

    def give_back(part):
        for target in range(GROUP):

            @pl.when(member != target)
            def _():
                for copy in back_copies(member, target, part):
                    copy.start()

            @pl.when(member == target)
            def _():
                for copy in kept_copies(target, part):
                    copy.start()

    def end_back(part):
        for target in range(GROUP):

            @pl.when(member != target)
            def _():
                for copy in back_copies(member, target, part):
                    copy.wait_send()

            @pl.when(member == target)
            def _():
                for copy in kept_copies(target, part):
                    copy.wait()
                for source in range(GROUP):
                    if source != target:
                        for copy in back_copies(source, target, part):
                            copy.wait_recv()

    def up_copy(source, target):
        start = OUTBOX + sum(UPS[:target])
        return remote(
            outbox.at[pl.ds(start, UPS[target])],
            parts.at[source, pl.ds(OWN * SPAN, UPS[target])],
            up_send.at[target],
            up_recv.at[source],
            base - GROUP + target,
        )

    for copy in mine:
        copy.wait()
    widen(member * OWN, OWN, 0)
    for k in (1, 2, 3):
        for copy in near[k - 1]:
            copy.wait_recv()
        who = other_member(member, k)
        pass_on(who, False)
        widen(who * OWN, OWN, 0)
    look_power(0)
    work(INSIDE, inside_pair)
    give_back(0)

    for source in range(GROUP):
        start, count, place, step = onward[source]
        gets = has_after if step < 0 else has_before

        @pl.when(gets)
        def _():
            for copy in far(source, False):
                copy.wait_recv()
            widen(place, count, LOCAL)

        @pl.when(jnp.logical_not(gets))
        def _():
            blank(place, count, LOCAL)

    look_power(LOCAL)
    work(RECT + 2 * FOLD, cross_pair)
    give_back(1)

    @pl.when(has_before)
    def _():
        for target in (2, 3):
            up_copy(member, target).start()

    for pair in near:
        for copy in pair:
            copy.wait_send()
    for source in range(GROUP):
        exists = has_before if onward[source][3] < 0 else has_after

        @pl.when(exists)
        def _():
            for copy in far(source, False):
                copy.wait_send()

    end_back(0)
    end_back(1)

    @pl.when(has_before)
    def _():
        for target in (2, 3):
            up_copy(member, target).wait_send()

    for target in (2, 3):

        @pl.when(jnp.logical_and(has_after, member == target))
        def _():
            for source in range(GROUP):
                up_copy(source, target).wait_recv()


def strip(acq, rim, win_rows, win_cols, groups):
    rows = acq.shape[2]
    width = acq.shape[3] // GROUP
    full = width + LANES
    out_rows = rows // STRIDE_R
    dates = (2, HELD, rows, full)
    smem = pl.BlockSpec(memory_space=pltpu.SMEM)
    hbm = pl.BlockSpec(memory_space=pl.ANY)
    dma = pltpu.SemaphoreType.DMA
    return pl.pallas_call(
        functools.partial(strip_kernel, groups, rows, width),
        out_shape=jax.ShapeDtypeStruct(
            (GROUP, OWN * SPAN + max(UPS), out_rows, LANES), jnp.float32
        ),
        in_specs=[smem, smem, hbm, hbm],
        out_specs=hbm,
        scratch_shapes=[
            pltpu.VMEM(dates, acq.dtype),
            pltpu.VMEM(dates, jnp.float32),
            pltpu.VMEM((2 * CHUNK * rows, full), jnp.bfloat16),
            pltpu.VMEM((full, LANES), jnp.bfloat16),
            pltpu.VMEM((CHUNK * out_rows, CHUNK * rows), jnp.bfloat16),
            pltpu.VMEM((2 * LOCAL, out_rows, LANES), jnp.float32),
            pltpu.VMEM((CHUNK, out_rows, LANES), jnp.float32),
            pltpu.VMEM((OUTBOX + FOLD, out_rows, LANES), jnp.float32),
            dma((GROUP, 2)),
            dma((GROUP, 2)),
            dma((GROUP, 2)),
            dma((GROUP, 2)),
            dma((2,)),
            dma((2, GROUP, OWN)),
            dma((2, GROUP, OWN)),
            dma((GROUP,)),
            dma((GROUP,)),
        ],
        compiler_params=pltpu.CompilerParams(
            collective_id=0, has_side_effects=True, vmem_limit_bytes=48 * 2**20
        ),
        name="strip",
    )(win_rows, win_cols, acq, rim)


def slots_kernel(count, pair_list, parts, out):
    date = lax.axis_index("date")
    member = date % GROUP
    half = LANES // 2
    left = lax.broadcasted_iota(jnp.int32, (parts.shape[2], LANES), 1) < half

    def one_slot(s, carry):
        i = pair_list[s, 0]
        alive = i >= 0
        step = i - date * OWN
        far = pair_list[s, 1] - i - 1
        at = step * SPAN + far
        size = member * OWN + step - DOWN
        later = size + far - SPAN
        gone = jnp.logical_and(size > 0, jnp.logical_and(later >= 0, later < size))
        first_up = jnp.maximum(member * OWN - DOWN, 1)
        behind = (size * (size - 1) - first_up * (first_up - 1)) // 2 + later
        at = jnp.where(gone, OWN * SPAN + behind, at)
        at = jnp.clip(jnp.where(alive, at, 0), 0, parts.shape[1] - 1)
        for n in range(GROUP // 2):
            a = parts[2 * n, at]
            b = parts[2 * n + 1, at]
            re = jnp.where(left, a, pltpu.roll(b, half, 1))
            im = jnp.where(left, pltpu.roll(a, half, 1), b)
            out[0, s, :, n * LANES : (n + 1) * LANES] = jnp.where(alive, re, 0.0)
            out[1, s, :, n * LANES : (n + 1) * LANES] = jnp.where(alive, im, 0.0)
        return carry

    lax.fori_loop(0, count, one_slot, 0)


def to_slots(pair_list, parts):
    count = pair_list.shape[0]
    smem = pl.BlockSpec(memory_space=pltpu.SMEM)
    vmem = pl.BlockSpec(memory_space=pltpu.VMEM)
    return pl.pallas_call(
        functools.partial(slots_kernel, count),
        out_shape=jax.ShapeDtypeStruct(
            (2, count, parts.shape[2], GROUP * LANES // 2), jnp.float32
        ),
        in_specs=[smem, vmem],
        out_specs=vmem,
        compiler_params=pltpu.CompilerParams(vmem_limit_bytes=16 * 2**20),
        name="to_slots",
    )(pair_list, parts)


def rims(acq):
    cols = acq.shape[3]
    width = cols // GROUP
    tile = lax.axis_index("tile")
    outgoing = jnp.where(tile == 0, acq[..., cols - HALF :], acq[..., :HALF])
    incoming = lax.ppermute(outgoing, "tile", [(0, 1), (1, 0)])
    nothing = jnp.zeros_like(incoming)
    lower = jnp.where(tile == 1, incoming, nothing)
    upper = jnp.where(tile == 0, incoming, nothing)
    pad = jnp.zeros((*acq.shape[:3], LANES - 2 * HALF), acq.dtype)
    pieces = []
    for k in range(GROUP):
        left = lower if k == 0 else acq[..., k * width - HALF : k * width]
        right = upper if k == GROUP - 1 else acq[..., (k + 1) * width : (k + 1) * width + HALF]
        pieces.append(jnp.concatenate((left, right, pad), axis=3))
    return jnp.stack(pieces)


def shards(groups, acquisitions, pair_list, win_rows, win_cols):
    parts = strip(acquisitions, rims(acquisitions), win_rows, win_cols, groups)
    return to_slots(pair_list, parts)


def solution(mesh):
    return jax.shard_map(
        functools.partial(shards, mesh.shape["date"] // GROUP),
        mesh=mesh,
        in_specs=(P(None, "date", "grp", "tile"), P("date", None), P(), P()),
        out_specs=P(None, "date", "grp", "tile"),
        check_vma=False,
    )
```

```python
import functools

import jax
import jax.numpy as jnp
from jax import lax
from jax.experimental import pallas as pl
from jax.experimental.pallas import tpu as pltpu
from jax.sharding import PartitionSpec as P

SPAN = 15
STRIDE_R = 4
STRIDE_C = 16
EPS = 1e-06

GROUP = 4
OWN = 4
LOCAL = GROUP * OWN
DOWN = 8
UP_FROM = DOWN + 1
UP = LOCAL - UP_FROM
HELD = LOCAL + DOWN + UP
HALF = STRIDE_C // 2
LANES = 128
PART = 16
CHUNK = 40
MESH = pl.DeviceIdType.MESH


INSIDE = LOCAL * (LOCAL - 1) // 2
RECT = (LOCAL - DOWN) * DOWN
FOLD = DOWN * (DOWN - 1) // 2
UPS = (0, 0, 6, 22)
OUTBOX = LOCAL * SPAN


def other_member(member, k):
    if k == 1:
        return member + 1 - 2 * (member % 2)
    if k == 2:
        return member + 2 - 4 * (member // 2)
    return GROUP - 1 - member


def inside_pair(f):
    x = lax.rem(f, LOCAL)
    y = x + lax.div(f, LOCAL) + 1
    turn = lax.div(y, LOCAL)
    i = x * (1 - turn) + (y - LOCAL) * turn
    j = y * (1 - turn) + x * turn
    return i, j, i * SPAN + j - i - 1


def cross_pair(f):
    beyond = lax.div(f, RECT)
    up = lax.div(f, RECT + FOLD)
    e = (f - RECT - FOLD * up) * beyond
    row = lax.div(e, DOWN - 1)
    col = lax.rem(e, DOWN - 1)
    turn = lax.div(col + row, DOWN - 1)
    size = (DOWN - 1 - row) * (1 - turn) + row * turn
    inner = col - (DOWN - 1 - row) * turn
    i = (1 - beyond) * (DOWN + lax.div(f, DOWN)) + (beyond - up) * size
    j = (1 - beyond) * lax.rem(f, DOWN) + (beyond - up) * inner + LOCAL
    i = (1 - up) * i + up * (LOCAL + DOWN + size - 1)
    j = (1 - up) * j + up * (DOWN + inner)
    near = i * SPAN + j - i - 1
    far = OUTBOX + lax.div(size * (size - 1), 2) + inner
    return i, j, (1 - up) * near + up * far


def split_dot(taps, values):
    high = values.astype(jnp.bfloat16)
    low = (values - high.astype(jnp.float32)).astype(jnp.bfloat16)
    return jnp.dot(taps, high, preferred_element_type=jnp.float32) + jnp.dot(
        taps, low, preferred_element_type=jnp.float32
    )


def strip_kernel(
    groups,
    rows,
    width,
    win_rows,
    win_cols,
    acq,
    rim,
    parts,
    held,
    wide,
    product,
    col_taps,
    row_taps,
    power,
    looked,
    outbox,
    send,
    recv,
    far_send,
    far_recv,
    local,
    back_send,
    back_recv,
    up_send,
    up_recv,
):
    out_rows = rows // STRIDE_R
    out_cols = width // STRIDE_C
    full = width + LANES
    cuts = range(0, full, 384)
    halves = rows // PART
    date = lax.axis_index("date")
    group, member = date // GROUP, date % GROUP
    base = group * GROUP
    has_before, has_after = group > 0, group < groups - 1
    is_late = member >= 2

    def greet(where):
        pl.semaphore_signal(
            pltpu.get_barrier_semaphore(),
            inc=1,
            device_id={"date": where},
            device_id_type=MESH,
        )

    for k in (1, 2, 3):
        greet(base + other_member(member, k))

    @pl.when(has_before)
    def _():
        greet(date - GROUP)
        for k in (2, 3):

            @pl.when(member != k)
            def _():
                greet(base - GROUP + k)

    @pl.when(has_after)
    def _():
        greet(date + GROUP)

        @pl.when(is_late)
        def _():
            for k in (1, 2, 3):
                greet(base + GROUP + other_member(member, k))

    late = member // 2
    peers = GROUP - 1 + has_before.astype(jnp.int32) * (3 - late)
    peers = peers + has_after.astype(jnp.int32) * (1 + 3 * late)
    pl.semaphore_wait(pltpu.get_barrier_semaphore(), peers)

    def body_of(who, h):
        columns = pl.ds(pl.multiple_of(who * width, width), width)
        return acq.at[:, :, pl.ds(h * PART, PART), columns]

    def rim_of(who, h):
        return rim.at[who, :, :, pl.ds(h * PART, PART)]

    def slot(start, count, h):
        part = held.at[:, pl.ds(start, count), pl.ds(h * PART, PART)]
        return part.at[:, :, :, pl.ds(0, width)], part.at[:, :, :, pl.ds(width, LANES)]

    def remote(src, dst, send_sem, recv_sem, where):
        return pltpu.make_async_remote_copy(
            src_ref=src,
            dst_ref=dst,
            send_sem=send_sem,
            recv_sem=recv_sem,
            device_id={"date": where},
            device_id_type=MESH,
        )

    onward = [
        (0, OWN, LOCAL, -1),
        (OWN, OWN, LOCAL + OWN, -1),
        (UP_FROM, 3 * OWN - UP_FROM, LOCAL + DOWN, 1),
        (3 * OWN, OWN, LOCAL + DOWN + 3 * OWN - UP_FROM, 1),
    ]

    def far(source, mine, h):
        start, count, place, step = onward[source]
        if mine:
            skip = start - source * OWN
            refs = (body_of(source, h), rim_of(source, h))
            srcs = [ref.at[:, pl.ds(skip, count)] for ref in refs]
        else:
            srcs = slot(start, count, h)
        return [
            remote(
                src,
                dst,
                far_send.at[h, source, n],
                far_recv.at[h, source, n],
                date + step * GROUP,
            )
            for n, (src, dst) in enumerate(zip(srcs, slot(place, count, h)))
        ]

    def pass_on(who, mine, h):
        for source in range(GROUP):
            exists = has_before if onward[source][3] < 0 else has_after

            @pl.when(jnp.logical_and(who == source, exists))
            def _():
                for copy in far(source, mine, h):
                    copy.start()

    def near(k, h):
        who = other_member(member, k)
        srcs = (body_of(who, h), rim_of(who, h))
        return [
            remote(src, dst, send.at[h, k, n], recv.at[h, k, n], base + who)
            for n, (src, dst) in enumerate(zip(srcs, slot(member * OWN, OWN, h)))
        ]

    def own(h):
        main, side = slot(member * OWN, OWN, h)
        return [
            pltpu.make_async_copy(body_of(member, h), main, local.at[h, 0]),
            pltpu.make_async_copy(rim_of(member, h), side, local.at[h, 1]),
        ]

    def send_near(k, h):
        for copy in near(k, h):
            copy.start()

    for k in (1, 2, 3):
        send_near(k, 0)
    pass_on(member, True, 0)
    for h in range(halves):
        for copy in own(h):
            copy.start()

    lane = lax.broadcasted_iota(jnp.int32, (full, LANES), 0)
    out = lax.broadcasted_iota(jnp.int32, (full, LANES), 1) % out_cols
    column = jnp.where(
        lane < width, lane, jnp.where(lane < width + HALF, lane - width - HALF, lane - HALF)
    )
    beside = jnp.abs(2 * column + 1 - (2 * out + 1) * STRIDE_C) <= win_cols[0]
    beside = jnp.logical_and(beside, lane < width + 2 * HALF)
    col_taps[...] = jnp.where(beside, 1.0, 0.0).astype(jnp.bfloat16)
    shape = (CHUNK * out_rows, CHUNK * PART)
    at = lax.broadcasted_iota(jnp.int32, shape, 0)
    row = lax.broadcasted_iota(jnp.int32, shape, 1)
    window = jnp.zeros(shape, jnp.int32)
    for o in range(out_rows):
        window = jnp.where(at % out_rows == o, win_rows[o], window)
    same = at // out_rows == row // PART
    for h in range(halves):
        reach = 2 * (row % PART + h * PART) + 1 - (2 * (at % out_rows) + 1) * STRIDE_R
        inside = jnp.logical_and(jnp.abs(reach) <= window, same)
        row_taps[h] = jnp.where(inside, 1.0, 0.0).astype(jnp.bfloat16)

    def widen(start, count, shift, h):
        low, high = h * PART, (h + 1) * PART

        def one_date(n, carry):
            d = start + n
            for c in cuts:
                re = held[0, d, low:high, c : c + 384].astype(jnp.float32)
                im = held[1, d, low:high, c : c + 384].astype(jnp.float32)
                wide[0, d, low:high, c : c + 384] = re
                wide[1, d, low:high, c : c + 384] = im
                to = pl.multiple_of((d - shift) * PART, PART)
                product[pl.ds(to, PART), c : c + 384] = (re * re + im * im).astype(jnp.bfloat16)
            return carry

        lax.fori_loop(0, count, one_date, 0)

    def blank(start, count, shift, h):
        def one_date(n, carry):
            d = start + n
            for part in range(2):
                wide[part, d, h * PART : (h + 1) * PART] = jnp.zeros((PART, full), jnp.float32)
            to = pl.multiple_of((d - shift) * PART, PART)
            product[pl.ds(to, PART), :] = jnp.zeros((PART, full), jnp.bfloat16)
            return carry

        lax.fori_loop(0, count, one_date, 0)

    def look_power(start, h):
        across = jnp.dot(
            product[: LOCAL * PART], col_taps[...], preferred_element_type=jnp.float32
        )
        taps = row_taps[h, : LOCAL * out_rows, : LOCAL * PART]
        sums = split_dot(taps, across).reshape(LOCAL, out_rows, LANES)
        if h:
            sums = sums + power[start : start + LOCAL]
        power[start : start + LOCAL] = sums

    def work(total, pair_of, h):
        low, high = h * PART, (h + 1) * PART

        def one_chunk(chunk, carry):
            def one_pair(p, carry):
                i, j, _ = pair_of(chunk * CHUNK + p)
                to = pl.multiple_of(p * 2 * PART, 2 * PART)
                for c in cuts:
                    re_i = wide[0, i, low:high, c : c + 384]
                    im_i = wide[1, i, low:high, c : c + 384]
                    re_j = wide[0, j, low:high, c : c + 384]
                    im_j = wide[1, j, low:high, c : c + 384]
                    re = (re_i * re_j + im_i * im_j).astype(jnp.bfloat16)
                    im = (im_i * re_j - re_i * im_j).astype(jnp.bfloat16)
                    product[pl.ds(to, PART), c : c + 384] = re
                    product[pl.ds(to + PART, PART), c : c + 384] = im
                return carry

            lax.fori_loop(0, CHUNK, one_pair, 0)
            across = jnp.dot(product[...], col_taps[...], preferred_element_type=jnp.float32)
            across = across.reshape(CHUNK, 2, PART, LANES)
            left = lax.broadcasted_iota(jnp.int32, (CHUNK, PART, LANES), 2) < out_cols
            both = jnp.where(left, across[:, 0], across[:, 1]).reshape(CHUNK * PART, LANES)
            looked[...] = split_dot(row_taps[h], both).reshape(CHUNK, out_rows, LANES)

            def finish(p, carry):
                i, j, to = pair_of(chunk * CHUNK + p)
                sums = looked[p]
                if h:
                    sums = sums + outbox[to]
                if h == halves - 1:
                    sums = sums * lax.rsqrt(power[i] * power[j] + EPS)
                outbox[to] = sums
                return carry

            lax.fori_loop(0, CHUNK, finish, 0)
            return carry

        lax.fori_loop(0, total // CHUNK, one_chunk, 0)

    def back(source, target, step, part):
        i = target * OWN + step
        if part == 0:
            start, count = 0, SPAN - i
        else:
            start, count = SPAN - i, min(i, DOWN)
        src = outbox.at[pl.ds(i * SPAN + start, count)]
        dst = parts.at[source, pl.ds(step * SPAN + start, count)]
        return src, dst, count

    def back_copies(source, target, part):
        copies = []
        for step in range(OWN):
            src, dst, count = back(source, target, step, part)
            if count:
                copies.append(
                    remote(
                        src,
                        dst,
                        back_send.at[part, target, step],
                        back_recv.at[part, source, step],
                        base + target,
                    )
                )
        return copies

    def kept_copies(target, part):
        copies = []
        for step in range(OWN):
            src, dst, count = back(target, target, step, part)
            if count:
                sem = back_send.at[part, target, step]
                copies.append(pltpu.make_async_copy(src, dst, sem))
        return copies

    def give_back(part):
        for target in range(GROUP):

            @pl.when(member != target)
            def _():
                for copy in back_copies(member, target, part):
                    copy.start()

            @pl.when(member == target)
            def _():
                for copy in kept_copies(target, part):
                    copy.start()

    def end_back(part):
        for target in range(GROUP):

            @pl.when(member != target)
            def _():
                for copy in back_copies(member, target, part):
                    copy.wait_send()

            @pl.when(member == target)
            def _():
                for copy in kept_copies(target, part):
                    copy.wait()
                for source in range(GROUP):
                    if source != target:
                        for copy in back_copies(source, target, part):
                            copy.wait_recv()

    def up_copy(source, target):
        start = OUTBOX + sum(UPS[:target])
        return remote(
            outbox.at[pl.ds(start, UPS[target])],
            parts.at[source, pl.ds(OWN * SPAN, UPS[target])],
            up_send.at[target],
            up_recv.at[source],
            base - GROUP + target,
        )

    def take_near(h):
        for copy in own(h):
            copy.wait()
        widen(member * OWN, OWN, 0, h)
        for k in (1, 2, 3):
            for copy in near(k, h):
                copy.wait_recv()
            who = other_member(member, k)
            pass_on(who, False, h)
            if h + 1 < halves:
                send_near(k, h + 1)
            widen(who * OWN, OWN, 0, h)
        if h + 1 < halves:
            pass_on(member, True, h + 1)
        look_power(0, h)

    def take_far(h):
        for source in range(GROUP):
            start, count, place, step = onward[source]
            gets = has_after if step < 0 else has_before

            @pl.when(gets)
            def _():
                for copy in far(source, False, h):
                    copy.wait_recv()
                widen(place, count, LOCAL, h)

            @pl.when(jnp.logical_not(gets))
            def _():
                blank(place, count, LOCAL, h)

        look_power(LOCAL, h)

    across_total = RECT + 2 * FOLD
    take_near(0)
    work(INSIDE, inside_pair, 0)
    for h in range(1, halves):
        take_near(h)
        take_far(h - 1)
        work(across_total, cross_pair, h - 1)
        work(INSIDE, inside_pair, h)
    give_back(0)
    take_far(halves - 1)
    work(across_total, cross_pair, halves - 1)
    give_back(1)

    @pl.when(has_before)
    def _():
        for target in (2, 3):
            up_copy(member, target).start()

    for h in range(halves):
        for k in (1, 2, 3):
            for copy in near(k, h):
                copy.wait_send()
        for source in range(GROUP):
            exists = has_before if onward[source][3] < 0 else has_after

            @pl.when(exists)
            def _():
                for copy in far(source, False, h):
                    copy.wait_send()

    end_back(0)
    end_back(1)

    @pl.when(has_before)
    def _():
        for target in (2, 3):
            up_copy(member, target).wait_send()

    for target in (2, 3):

        @pl.when(jnp.logical_and(has_after, member == target))
        def _():
            for source in range(GROUP):
                up_copy(source, target).wait_recv()


def strip(acq, rim, win_rows, win_cols, groups):
    rows = acq.shape[2]
    width = acq.shape[3] // GROUP
    full = width + LANES
    out_rows = rows // STRIDE_R
    dates = (2, HELD, rows, full)
    halves = rows // PART
    smem = pl.BlockSpec(memory_space=pltpu.SMEM)
    hbm = pl.BlockSpec(memory_space=pl.ANY)
    dma = pltpu.SemaphoreType.DMA
    return pl.pallas_call(
        functools.partial(strip_kernel, groups, rows, width),
        out_shape=jax.ShapeDtypeStruct(
            (GROUP, OWN * SPAN + max(UPS), out_rows, LANES), jnp.float32
        ),
        in_specs=[smem, smem, hbm, hbm],
        out_specs=hbm,
        scratch_shapes=[
            pltpu.VMEM(dates, acq.dtype),
            pltpu.VMEM(dates, jnp.float32),
            pltpu.VMEM((2 * CHUNK * PART, full), jnp.bfloat16),
            pltpu.VMEM((full, LANES), jnp.bfloat16),
            pltpu.VMEM((halves, CHUNK * out_rows, CHUNK * PART), jnp.bfloat16),
            pltpu.VMEM((2 * LOCAL, out_rows, LANES), jnp.float32),
            pltpu.VMEM((CHUNK, out_rows, LANES), jnp.float32),
            pltpu.VMEM((OUTBOX + FOLD, out_rows, LANES), jnp.float32),
            dma((halves, GROUP, 2)),
            dma((halves, GROUP, 2)),
            dma((halves, GROUP, 2)),
            dma((halves, GROUP, 2)),
            dma((halves, 2)),
            dma((2, GROUP, OWN)),
            dma((2, GROUP, OWN)),
            dma((GROUP,)),
            dma((GROUP,)),
        ],
        compiler_params=pltpu.CompilerParams(
            collective_id=0, has_side_effects=True, vmem_limit_bytes=48 * 2**20
        ),
        name="strip",
    )(win_rows, win_cols, acq, rim)


def slots_kernel(count, pair_list, parts, out):
    date = lax.axis_index("date")
    member = date % GROUP
    half = LANES // 2
    left = lax.broadcasted_iota(jnp.int32, (parts.shape[2], LANES), 1) < half

    def one_slot(s, carry):
        i = pair_list[s, 0]
        alive = i >= 0
        step = i - date * OWN
        far = pair_list[s, 1] - i - 1
        at = step * SPAN + far
        size = member * OWN + step - DOWN
        later = size + far - SPAN
        gone = jnp.logical_and(size > 0, jnp.logical_and(later >= 0, later < size))
        first_up = jnp.maximum(member * OWN - DOWN, 1)
        behind = (size * (size - 1) - first_up * (first_up - 1)) // 2 + later
        at = jnp.where(gone, OWN * SPAN + behind, at)
        at = jnp.clip(jnp.where(alive, at, 0), 0, parts.shape[1] - 1)
        for n in range(GROUP // 2):
            a = parts[2 * n, at]
            b = parts[2 * n + 1, at]
            re = jnp.where(left, a, pltpu.roll(b, half, 1))
            im = jnp.where(left, pltpu.roll(a, half, 1), b)
            out[0, s, :, n * LANES : (n + 1) * LANES] = jnp.where(alive, re, 0.0)
            out[1, s, :, n * LANES : (n + 1) * LANES] = jnp.where(alive, im, 0.0)
        return carry

    lax.fori_loop(0, count, one_slot, 0)


def to_slots(pair_list, parts):
    count = pair_list.shape[0]
    smem = pl.BlockSpec(memory_space=pltpu.SMEM)
    vmem = pl.BlockSpec(memory_space=pltpu.VMEM)
    return pl.pallas_call(
        functools.partial(slots_kernel, count),
        out_shape=jax.ShapeDtypeStruct(
            (2, count, parts.shape[2], GROUP * LANES // 2), jnp.float32
        ),
        in_specs=[smem, vmem],
        out_specs=vmem,
        compiler_params=pltpu.CompilerParams(vmem_limit_bytes=16 * 2**20),
        name="to_slots",
    )(pair_list, parts)


def rims(acq):
    cols = acq.shape[3]
    width = cols // GROUP
    tile = lax.axis_index("tile")
    outgoing = jnp.where(tile == 0, acq[..., cols - HALF :], acq[..., :HALF])
    incoming = lax.ppermute(outgoing, "tile", [(0, 1), (1, 0)])
    nothing = jnp.zeros_like(incoming)
    lower = jnp.where(tile == 1, incoming, nothing)
    upper = jnp.where(tile == 0, incoming, nothing)
    pad = jnp.zeros((*acq.shape[:3], LANES - 2 * HALF), acq.dtype)
    pieces = []
    for k in range(GROUP):
        left = lower if k == 0 else acq[..., k * width - HALF : k * width]
        right = upper if k == GROUP - 1 else acq[..., (k + 1) * width : (k + 1) * width + HALF]
        pieces.append(jnp.concatenate((left, right, pad), axis=3))
    return jnp.stack(pieces)


def shards(groups, acquisitions, pair_list, win_rows, win_cols):
    parts = strip(acquisitions, rims(acquisitions), win_rows, win_cols, groups)
    return to_slots(pair_list, parts)


def solution(mesh):
    return jax.shard_map(
        functools.partial(shards, mesh.shape["date"] // GROUP),
        mesh=mesh,
        in_specs=(P(None, "date", "grp", "tile"), P("date", None), P(), P()),
        out_specs=P(None, "date", "grp", "tile"),
        check_vma=False,
    )
```

```python
import functools

import jax
import jax.numpy as jnp
from jax import lax
from jax.experimental import pallas as pl
from jax.experimental.pallas import tpu as pltpu
from jax.sharding import PartitionSpec as P

SPAN = 15
STRIDE_R = 4
STRIDE_C = 16
EPS = 1e-06

GROUP = 4
OWN = 4
LOCAL = GROUP * OWN
DOWN = 8
UP_FROM = DOWN + 1
UP = LOCAL - UP_FROM
HELD = LOCAL + DOWN + UP
HALF = STRIDE_C // 2
LANES = 128
CHUNK = 24
MESH = pl.DeviceIdType.MESH


INSIDE = LOCAL * (LOCAL - 1) // 2
RECT = (LOCAL - DOWN) * DOWN
FOLD = DOWN * (DOWN - 1) // 2
UPS = (0, 0, 6, 22)
OUTBOX = LOCAL * SPAN


def other_member(member, k):
    if k == 1:
        return member + 1 - 2 * (member % 2)
    if k == 2:
        return member + 2 - 4 * (member // 2)
    return GROUP - 1 - member


def inside_pair(f):
    x = lax.rem(f, LOCAL)
    y = x + lax.div(f, LOCAL) + 1
    turn = lax.div(y, LOCAL)
    i = x * (1 - turn) + (y - LOCAL) * turn
    j = y * (1 - turn) + x * turn
    return i, j, i * SPAN + j - i - 1


def cross_pair(f):
    beyond = lax.div(f, RECT)
    up = lax.div(f, RECT + FOLD)
    e = (f - RECT - FOLD * up) * beyond
    row = lax.div(e, DOWN - 1)
    col = lax.rem(e, DOWN - 1)
    turn = lax.div(col + row, DOWN - 1)
    size = (DOWN - 1 - row) * (1 - turn) + row * turn
    inner = col - (DOWN - 1 - row) * turn
    i = (1 - beyond) * (DOWN + lax.div(f, DOWN)) + (beyond - up) * size
    j = (1 - beyond) * lax.rem(f, DOWN) + (beyond - up) * inner + LOCAL
    i = (1 - up) * i + up * (LOCAL + DOWN + size - 1)
    j = (1 - up) * j + up * (DOWN + inner)
    near = i * SPAN + j - i - 1
    far = OUTBOX + lax.div(size * (size - 1), 2) + inner
    return i, j, (1 - up) * near + up * far


def split_dot(taps, values):
    high = values.astype(jnp.bfloat16)
    low = (values - high.astype(jnp.float32)).astype(jnp.bfloat16)
    return jnp.dot(taps, high, preferred_element_type=jnp.float32) + jnp.dot(
        taps, low, preferred_element_type=jnp.float32
    )


def strip_kernel(
    groups,
    rows,
    width,
    win_rows,
    win_cols,
    acq,
    rim,
    parts,
    held,
    wide,
    product,
    col_taps,
    row_taps,
    power,
    looked,
    outbox,
    send,
    recv,
    far_send,
    far_recv,
    local,
    back_send,
    back_recv,
    up_send,
    up_recv,
):
    out_rows = rows // STRIDE_R
    out_cols = width // STRIDE_C
    full = width + LANES
    cuts = [(r, c) for r in range(0, rows, 16) for c in range(0, full, 384)]
    date = lax.axis_index("date")
    group, member = date // GROUP, date % GROUP
    base = group * GROUP
    has_before, has_after = group > 0, group < groups - 1
    is_late = member >= 2

    def greet(where):
        pl.semaphore_signal(
            pltpu.get_barrier_semaphore(),
            inc=1,
            device_id={"date": where},
            device_id_type=MESH,
        )

    for k in (1, 2, 3):
        greet(base + other_member(member, k))

    @pl.when(has_before)
    def _():
        greet(date - GROUP)
        for k in (2, 3):

            @pl.when(member != k)
            def _():
                greet(base - GROUP + k)

    @pl.when(has_after)
    def _():
        greet(date + GROUP)

        @pl.when(is_late)
        def _():
            for k in (1, 2, 3):
                greet(base + GROUP + other_member(member, k))

    late = member // 2
    peers = GROUP - 1 + has_before.astype(jnp.int32) * (3 - late)
    peers = peers + has_after.astype(jnp.int32) * (1 + 3 * late)
    pl.semaphore_wait(pltpu.get_barrier_semaphore(), peers)

    def body_of(who):
        return acq.at[:, :, :, pl.ds(pl.multiple_of(who * width, width), width)]

    def rim_of(who):
        return rim.at[who]

    def slot(start, count):
        part = held.at[:, pl.ds(start, count)]
        return part.at[:, :, :, pl.ds(0, width)], part.at[:, :, :, pl.ds(width, LANES)]

    def remote(src, dst, send_sem, recv_sem, where):
        return pltpu.make_async_remote_copy(
            src_ref=src,
            dst_ref=dst,
            send_sem=send_sem,
            recv_sem=recv_sem,
            device_id={"date": where},
            device_id_type=MESH,
        )

    onward = [
        (0, OWN, LOCAL, -1),
        (OWN, OWN, LOCAL + OWN, -1),
        (UP_FROM, 3 * OWN - UP_FROM, LOCAL + DOWN, 1),
        (3 * OWN, OWN, LOCAL + DOWN + 3 * OWN - UP_FROM, 1),
    ]

    def far(source, mine):
        start, count, place, step = onward[source]
        if mine:
            skip = start - source * OWN
            srcs = [ref.at[:, pl.ds(skip, count)] for ref in (body_of(source), rim_of(source))]
        else:
            srcs = slot(start, count)
        return [
            remote(
                src, dst, far_send.at[source, n], far_recv.at[source, n], date + step * GROUP
            )
            for n, (src, dst) in enumerate(zip(srcs, slot(place, count)))
        ]

    def pass_on(who, mine):
        for source in range(GROUP):
            exists = has_before if onward[source][3] < 0 else has_after

            @pl.when(jnp.logical_and(who == source, exists))
            def _():
                for copy in far(source, mine):
                    copy.start()

    near = []
    for k in (1, 2, 3):
        who = other_member(member, k)
        pair = [
            remote(src, dst, send.at[k, n], recv.at[k, n], base + who)
            for n, (src, dst) in enumerate(
                zip((body_of(who), rim_of(who)), slot(member * OWN, OWN))
            )
        ]
        for copy in pair:
            copy.start()
        near.append(pair)
    pass_on(member, True)
    main, side = slot(member * OWN, OWN)
    mine = [
        pltpu.make_async_copy(body_of(member), main, local.at[0]),
        pltpu.make_async_copy(rim_of(member), side, local.at[1]),
    ]
    for copy in mine:
        copy.start()

    lane = lax.broadcasted_iota(jnp.int32, (full, LANES), 0)
    out = lax.broadcasted_iota(jnp.int32, (full, LANES), 1) % out_cols
    column = jnp.where(
        lane < width, lane, jnp.where(lane < width + HALF, lane - width - HALF, lane - HALF)
    )
    beside = jnp.abs(2 * column + 1 - (2 * out + 1) * STRIDE_C) <= win_cols[0]
    beside = jnp.logical_and(beside, lane < width + 2 * HALF)
    col_taps[...] = jnp.where(beside, 1.0, 0.0).astype(jnp.bfloat16)
    shape = (CHUNK * out_rows, CHUNK * rows)
    at = lax.broadcasted_iota(jnp.int32, shape, 0)
    row = lax.broadcasted_iota(jnp.int32, shape, 1)
    window = jnp.zeros(shape, jnp.int32)
    for o in range(out_rows):
        window = jnp.where(at % out_rows == o, win_rows[o], window)
    inside = jnp.abs(2 * (row % rows) + 1 - (2 * (at % out_rows) + 1) * STRIDE_R) <= window
    inside = jnp.logical_and(inside, at // out_rows == row // rows)
    row_taps[...] = jnp.where(inside, 1.0, 0.0).astype(jnp.bfloat16)

    def widen(start, count, shift):
        def one_date(n, carry):
            d = start + n
            for r, c in cuts:
                re = held[0, d, r : r + 16, c : c + 384].astype(jnp.float32)
                im = held[1, d, r : r + 16, c : c + 384].astype(jnp.float32)
                wide[0, d, r : r + 16, c : c + 384] = re
                wide[1, d, r : r + 16, c : c + 384] = im
                to = pl.multiple_of((d - shift) * rows + r, 16)
                product[pl.ds(to, 16), c : c + 384] = (re * re + im * im).astype(jnp.bfloat16)
            return carry

        lax.fori_loop(0, count, one_date, 0)

    def blank(start, count, shift):
        def one_date(n, carry):
            d = start + n
            for part in range(2):
                wide[part, d] = jnp.zeros((rows, full), jnp.float32)
            to = pl.multiple_of((d - shift) * rows, 16)
            product[pl.ds(to, rows), :] = jnp.zeros((rows, full), jnp.bfloat16)
            return carry

        lax.fori_loop(0, count, one_date, 0)

    def look_power(start):
        across = jnp.dot(
            product[: LOCAL * rows], col_taps[...], preferred_element_type=jnp.float32
        )
        taps = row_taps[: LOCAL * out_rows, : LOCAL * rows]
        power[start : start + LOCAL] = split_dot(taps, across).reshape(LOCAL, out_rows, LANES)

    def work(total, pair_of):
        def one_chunk(chunk, carry):
            def one_pair(p, carry):
                i, j, _ = pair_of(chunk * CHUNK + p)
                for r, c in cuts:
                    re_i = wide[0, i, r : r + 16, c : c + 384]
                    im_i = wide[1, i, r : r + 16, c : c + 384]
                    re_j = wide[0, j, r : r + 16, c : c + 384]
                    im_j = wide[1, j, r : r + 16, c : c + 384]
                    re = (re_i * re_j + im_i * im_j).astype(jnp.bfloat16)
                    im = (im_i * re_j - re_i * im_j).astype(jnp.bfloat16)
                    product[pl.ds(pl.multiple_of(p * 2 * rows + r, 16), 16), c : c + 384] = re
                    at = pl.multiple_of(p * 2 * rows + rows + r, 16)
                    product[pl.ds(at, 16), c : c + 384] = im
                return carry

            lax.fori_loop(0, CHUNK, one_pair, 0, unroll=2)
            across = jnp.dot(product[...], col_taps[...], preferred_element_type=jnp.float32)
            across = across.reshape(CHUNK, 2, rows, LANES)
            left = lax.broadcasted_iota(jnp.int32, (CHUNK, rows, LANES), 2) < out_cols
            both = jnp.where(left, across[:, 0], across[:, 1]).reshape(CHUNK * rows, LANES)
            looked[...] = split_dot(row_taps[...], both).reshape(CHUNK, out_rows, LANES)

            def finish(p, carry):
                i, j, to = pair_of(chunk * CHUNK + p)
                outbox[to] = looked[p] * lax.rsqrt(power[i] * power[j] + EPS)
                return carry

            lax.fori_loop(0, CHUNK, finish, 0, unroll=8)
            return carry

        lax.fori_loop(0, total // CHUNK, one_chunk, 0)

    def back(source, target, step, part):
        i = target * OWN + step
        if part == 0:
            start, count = 0, SPAN - i
        else:
            start, count = SPAN - i, min(i, DOWN)
        src = outbox.at[pl.ds(i * SPAN + start, count)]
        dst = parts.at[source, pl.ds(step * SPAN + start, count)]
        return src, dst, count

    def back_copies(source, target, part):
        copies = []
        for step in range(OWN):
            src, dst, count = back(source, target, step, part)
            if count:
                copies.append(
                    remote(
                        src,
                        dst,
                        back_send.at[part, target, step],
                        back_recv.at[part, source, step],
                        base + target,
                    )
                )
        return copies

    def kept_copies(target, part):
        copies = []
        for step in range(OWN):
            src, dst, count = back(target, target, step, part)
            if count:
                sem = back_send.at[part, target, step]
                copies.append(pltpu.make_async_copy(src, dst, sem))
        return copies

    def give_back(part):
        for target in range(GROUP):

            @pl.when(member != target)
            def _():
                for copy in back_copies(member, target, part):
                    copy.start()

            @pl.when(member == target)
            def _():
                for copy in kept_copies(target, part):
                    copy.start()

    def end_back(part):
        for target in range(GROUP):

            @pl.when(member != target)
            def _():
                for copy in back_copies(member, target, part):
                    copy.wait_send()

            @pl.when(member == target)
            def _():
                for copy in kept_copies(target, part):
                    copy.wait()
                for source in range(GROUP):
                    if source != target:
                        for copy in back_copies(source, target, part):
                            copy.wait_recv()

    def up_copy(source, target):
        start = OUTBOX + sum(UPS[:target])
        return remote(
            outbox.at[pl.ds(start, UPS[target])],
            parts.at[source, pl.ds(OWN * SPAN, UPS[target])],
            up_send.at[target],
            up_recv.at[source],
            base - GROUP + target,
        )

    for copy in mine:
        copy.wait()
    widen(member * OWN, OWN, 0)
    for k in (1, 2, 3):
        for copy in near[k - 1]:
            copy.wait_recv()
        who = other_member(member, k)
        pass_on(who, False)
        widen(who * OWN, OWN, 0)
    look_power(0)
    work(INSIDE, inside_pair)
    give_back(0)

    for source in range(GROUP):
        start, count, place, step = onward[source]
        gets = has_after if step < 0 else has_before

        @pl.when(gets)
        def _():
            for copy in far(source, False):
                copy.wait_recv()
            widen(place, count, LOCAL)

        @pl.when(jnp.logical_not(gets))
        def _():
            blank(place, count, LOCAL)

    look_power(LOCAL)
    work(RECT + 2 * FOLD, cross_pair)
    give_back(1)

    @pl.when(has_before)
    def _():
        for target in (2, 3):
            up_copy(member, target).start()

    for pair in near:
        for copy in pair:
            copy.wait_send()
    for source in range(GROUP):
        exists = has_before if onward[source][3] < 0 else has_after

        @pl.when(exists)
        def _():
            for copy in far(source, False):
                copy.wait_send()

    end_back(0)
    end_back(1)

    @pl.when(has_before)
    def _():
        for target in (2, 3):
            up_copy(member, target).wait_send()

    for target in (2, 3):

        @pl.when(jnp.logical_and(has_after, member == target))
        def _():
            for source in range(GROUP):
                up_copy(source, target).wait_recv()


def strip(acq, rim, win_rows, win_cols, groups):
    rows = acq.shape[2]
    width = acq.shape[3] // GROUP
    full = width + LANES
    out_rows = rows // STRIDE_R
    dates = (2, HELD, rows, full)
    smem = pl.BlockSpec(memory_space=pltpu.SMEM)
    hbm = pl.BlockSpec(memory_space=pl.ANY)
    dma = pltpu.SemaphoreType.DMA
    return pl.pallas_call(
        functools.partial(strip_kernel, groups, rows, width),
        out_shape=jax.ShapeDtypeStruct(
            (GROUP, OWN * SPAN + max(UPS), out_rows, LANES), jnp.float32
        ),
        in_specs=[smem, smem, hbm, hbm],
        out_specs=hbm,
        scratch_shapes=[
            pltpu.VMEM(dates, acq.dtype),
            pltpu.VMEM(dates, jnp.float32),
            pltpu.VMEM((2 * CHUNK * rows, full), jnp.bfloat16),
            pltpu.VMEM((full, LANES), jnp.bfloat16),
            pltpu.VMEM((CHUNK * out_rows, CHUNK * rows), jnp.bfloat16),
            pltpu.VMEM((2 * LOCAL, out_rows, LANES), jnp.float32),
            pltpu.VMEM((CHUNK, out_rows, LANES), jnp.float32),
            pltpu.VMEM((OUTBOX + FOLD, out_rows, LANES), jnp.float32),
            dma((GROUP, 2)),
            dma((GROUP, 2)),
            dma((GROUP, 2)),
            dma((GROUP, 2)),
            dma((2,)),
            dma((2, GROUP, OWN)),
            dma((2, GROUP, OWN)),
            dma((GROUP,)),
            dma((GROUP,)),
        ],
        compiler_params=pltpu.CompilerParams(
            collective_id=0, has_side_effects=True, vmem_limit_bytes=48 * 2**20
        ),
        name="strip",
    )(win_rows, win_cols, acq, rim)


def slots_kernel(count, pair_list, parts, out):
    date = lax.axis_index("date")
    member = date % GROUP
    half = LANES // 2
    left = lax.broadcasted_iota(jnp.int32, (parts.shape[2], LANES), 1) < half

    def one_slot(s, carry):
        i = pair_list[s, 0]
        alive = i >= 0
        step = i - date * OWN
        far = pair_list[s, 1] - i - 1
        at = step * SPAN + far
        size = member * OWN + step - DOWN
        later = size + far - SPAN
        gone = jnp.logical_and(size > 0, jnp.logical_and(later >= 0, later < size))
        first_up = jnp.maximum(member * OWN - DOWN, 1)
        behind = (size * (size - 1) - first_up * (first_up - 1)) // 2 + later
        at = jnp.where(gone, OWN * SPAN + behind, at)
        at = jnp.clip(jnp.where(alive, at, 0), 0, parts.shape[1] - 1)
        for n in range(GROUP // 2):
            a = parts[2 * n, at]
            b = parts[2 * n + 1, at]
            re = jnp.where(left, a, pltpu.roll(b, half, 1))
            im = jnp.where(left, pltpu.roll(a, half, 1), b)
            out[0, s, :, n * LANES : (n + 1) * LANES] = jnp.where(alive, re, 0.0)
            out[1, s, :, n * LANES : (n + 1) * LANES] = jnp.where(alive, im, 0.0)
        return carry

    lax.fori_loop(0, count, one_slot, 0, unroll=6)


def to_slots(pair_list, parts):
    count = pair_list.shape[0]
    smem = pl.BlockSpec(memory_space=pltpu.SMEM)
    vmem = pl.BlockSpec(memory_space=pltpu.VMEM)
    return pl.pallas_call(
        functools.partial(slots_kernel, count),
        out_shape=jax.ShapeDtypeStruct(
            (2, count, parts.shape[2], GROUP * LANES // 2), jnp.float32
        ),
        in_specs=[smem, vmem],
        out_specs=vmem,
        compiler_params=pltpu.CompilerParams(vmem_limit_bytes=16 * 2**20),
        name="to_slots",
    )(pair_list, parts)


def rims(acq):
    cols = acq.shape[3]
    width = cols // GROUP
    tile = lax.axis_index("tile")
    outgoing = jnp.where(tile == 0, acq[..., cols - HALF :], acq[..., :HALF])
    incoming = lax.ppermute(outgoing, "tile", [(0, 1), (1, 0)])
    nothing = jnp.zeros_like(incoming)
    lower = jnp.where(tile == 1, incoming, nothing)
    upper = jnp.where(tile == 0, incoming, nothing)
    pad = jnp.zeros((*acq.shape[:3], LANES - 2 * HALF), acq.dtype)
    pieces = []
    for k in range(GROUP):
        left = lower if k == 0 else acq[..., k * width - HALF : k * width]
        right = upper if k == GROUP - 1 else acq[..., (k + 1) * width : (k + 1) * width + HALF]
        pieces.append(jnp.concatenate((left, right, pad), axis=3))
    return jnp.stack(pieces)


def shards(groups, acquisitions, pair_list, win_rows, win_cols):
    parts = strip(acquisitions, rims(acquisitions), win_rows, win_cols, groups)
    return to_slots(pair_list, parts)


def solution(mesh):
    return jax.shard_map(
        functools.partial(shards, mesh.shape["date"] // GROUP),
        mesh=mesh,
        in_specs=(P(None, "date", "grp", "tile"), P("date", None), P(), P()),
        out_specs=P(None, "date", "grp", "tile"),
        check_vma=False,
    )
```
